32 devices in a mesh: gx: 8 (over y, x, core), gy: 4 (over z).
Axes of the slice: x: 2, y: 2, z: 4, core: 2. Of those that a mesh axis runs over, the one named last changes fastest.
Arguments:
- node_values: bfloat16 [24, 12, 128, 256], P('gx', 'gy'), may hold values from -6 to 6
- fit_ops: bfloat16 [8, 4, 8, 320, 300], P('gx', 'gy'), may hold values from -0.0034179688 to 0.0034179688
- node_xyz: float32 [8, 4, 8, 3, 300], P('gx', 'gy'), may hold values from -6 to 6
- patch_nodes: int32 [8, 4, 8, 300], P('gx', 'gy'), may hold values from 0 to 3199, as said below
- patch_valid: int32 [8, 4, 8], P('gx', 'gy'), may hold values from 160 to 300
- patch_cell: int32 [8, 4, 8, 3], P('gx', 'gy'), may hold values from 0 to 11, as said below
- patch_radius: float32 [8, 4, 8], P('gx', 'gy'), may hold values from 3 to 6
- cell_scale: float32 [96, 48, 8], P('gx', 'gy'), may hold values from 0.5 to 2
Outputs:
- velocity: bfloat16 [96, 48, 8, 256], P('gx', 'gy')
The draws below stay inside these ranges and needn't reach their ends.
Inputs may be any that keep to these rules, and one draw needn't show every extreme that they name: `patch_nodes`: an entry (a * 5 + b) * 128 + n names node n of subregion (a, b) among the 5 by 5 subregions around the patch's tile, whose own subregions are a, b = 1 to 3; a and b differ by at most one from the subregion 1 + (3 c0) // 12, 1 + (3 c1) // 12 that holds the patch's centre cell, and the subregion never lies outside the grid along the second horizontal dimension. `patch_cell`: the first entry is below 12, the second below 12, the third at most 4.
All inputs are finite; a program needn't handle non-finite values.
Results may differ from the reference program's by a relative error of at most 0.0085.
Values may be sent and summed in bfloat16 or wider, within the bound.
No kernel may reach another device: no remote copies, remote signals or barrier semaphores. Data moves between devices by JAX's collectives and lax.ppermute only.
A program may use at most 64 MiB of HBM per device.

```python
import math
import jax
import jax.numpy as jnp
import numpy as np
from jax import lax

K = 300
KP = 320
F = 256
NSUB = 128
PATCH_DEV = 8
CX = 12
CY = 12
CZ = 8
TILES_X = 8
TILES_Y = 4
NX = 96
NY = 48


def centres(key):
    base = jax.random.fold_in(key, 7)
    first_key, second_key, third_key = jax.random.split(base, 3)
    shape = (TILES_X, TILES_Y, PATCH_DEV)
    first = jax.random.randint(first_key, shape, 0, CX, dtype=jnp.int32)
    second = jax.random.randint(second_key, shape, 0, CY, dtype=jnp.int32)
    third = jax.random.randint(third_key, shape, 0, CZ - 3, dtype=jnp.int32)
    return (first, second, third)


def draw_patch_cell(key, part):
    first, second, third = centres(key)
    return jnp.stack([first, second, third], -1).astype(jnp.int32)


def draw_patch_nodes(key, part):
    first, second, third = centres(key)
    shape = (TILES_X, TILES_Y, PATCH_DEV, K)
    across_key, along_key, node_key = jax.random.split(jax.random.fold_in(key, 11), 3)
    home_x = 3 * first // CX
    home_y = 3 * second // CY
    sub_x = home_x[..., None] + jax.random.randint(across_key, shape, 0, 3, dtype=jnp.int32)
    sub_y = home_y[..., None] + jax.random.randint(along_key, shape, 0, 3, dtype=jnp.int32)
    tile_y = lax.broadcasted_iota(jnp.int32, shape, 1)
    lowest = jnp.where(tile_y == 0, 1, 0).astype(jnp.int32)
    highest = jnp.where(tile_y == TILES_Y - 1, 3, 4).astype(jnp.int32)
    sub_y = jnp.minimum(jnp.maximum(sub_y, lowest), highest)
    node = jax.random.randint(node_key, shape, 0, NSUB, dtype=jnp.int32)
    return ((sub_x * 5 + sub_y) * NSUB + node).astype(jnp.int32)


def set_ends(drawn, own_key, smallest, top_value):
    longest = drawn.shape.index(max(drawn.shape))
    spots = []
    for shift in (0, 1):
        where = [jax.random.randint(jax.random.fold_in(own_key, axis), (), 0, length) for axis, length in enumerate(drawn.shape)]
        where[longest] = (where[longest] + shift) % drawn.shape[longest]
        spots.append(tuple(where))
    return drawn.at[spots[0]].set(smallest).at[spots[1]].set(top_value)


def shard_levels(rng, shape, cuts, smallest, top_value):
    def one(position, parts):
        heights = jax.random.uniform(jax.random.fold_in(jax.random.fold_in(rng, 6), position), (parts,), jnp.float32, smallest / len(cuts), top_value / len(cuts))
        return jnp.repeat(jnp.exp(heights), shape[position] // parts).reshape((-1,) + (1,) * (len(shape) - position - 1))

    gain = one(*cuts[0])
    for cut in cuts[1:]:
        gain = gain * one(*cut)
    return gain


def noise(own_key, shape, spread, most, cuts=(), kind=jnp.bfloat16):
    result = jax.random.normal(own_key, shape, jnp.float32) * spread
    if len(cuts) > 0:
        result = shard_levels(own_key, shape, cuts, -0.22, 0.18) * result
    return jnp.clip(result, min=-most, max=most).astype(kind)


def setup_inputs(seed: int = 0) -> dict:
    key_list = jax.random.split(jax.random.key(seed), 9)
    return {
        "node_values": noise(key_list[0], (3 * TILES_X, 3 * TILES_Y, NSUB, F), 1.0, 6.0, ((0, 8), (1, 4))),
        "fit_ops": noise(key_list[1], (TILES_X, TILES_Y, PATCH_DEV, KP, K), (36 * K * K) ** -0.5, 0.0034179688, ((0, 8), (1, 4))),
        "node_xyz": jnp.clip(jax.random.uniform(key_list[2], (TILES_X, TILES_Y, PATCH_DEV, 3, K), jnp.float32, -6.0, 6.0) * shard_levels(key_list[2], (TILES_X, TILES_Y, PATCH_DEV, 3, K), ((0, 8), (1, 4)), -0.4, 0.0), -6.0, 6.0),
        "patch_nodes": draw_patch_nodes(jax.random.fold_in(key_list[8], 71), 0),
        "patch_valid": set_ends(jax.random.randint(key_list[4], (TILES_X, TILES_Y, PATCH_DEV), K // 2 + 10, K + 1), jax.random.fold_in(key_list[4], 1), K // 2 + 10, K).astype(jnp.int32),
        "patch_cell": draw_patch_cell(jax.random.fold_in(key_list[8], 71), 0),
        "patch_radius": jnp.clip(jnp.exp(math.log(6.0) - 0.6931472 * jax.random.uniform(key_list[6], (TILES_X, TILES_Y, PATCH_DEV), jnp.float32) ** shard_levels(key_list[6], (TILES_X, TILES_Y, PATCH_DEV), ((0, 8), (1, 4)), -0.2, 0.2)), 3.0, 6.0),
        "cell_scale": jnp.clip(jnp.exp(math.log(2.0) - 1.3862944 * jax.random.uniform(key_list[7], (NX, NY, CZ), jnp.float32) ** shard_levels(key_list[7], (NX, NY, CZ), ((0, 8), (1, 4)), -0.2, 0.2)), 0.5, 2.0),
    }


EXPONENTS = ((0, 0, 0), (1, 0, 0), (0, 1, 0), (0, 0, 1), (2, 0, 0), (1, 1, 0), (1, 0, 1), (0, 2, 0), (0, 1, 1), (0, 0, 2), (3, 0, 0), (2, 1, 0), (2, 0, 1), (1, 2, 0), (1, 1, 1), (1, 0, 2), (0, 3, 0), (0, 2, 1), (0, 1, 2), (0, 0, 3))

def stencil():
    across = np.arange(-4, 5).astype(np.float32)
    depth = np.arange(4).astype(np.float32) - 1.5
    first, second, third = np.meshgrid(across, across, depth, indexing='ij')
    return np.stack([first.ravel(), second.ravel(), third.ravel()], 1).astype(np.float32)

def patch_terms(gathered, operators, xyz, valid, radius):
    count = gathered.shape[0]
    fields = gathered.shape[2]
    slots = lax.broadcasted_iota(jnp.int32, gathered.shape[:2], 1)
    masked = jnp.where((slots < valid[:, None])[:, :, None], gathered, jnp.zeros((), gathered.dtype))
    coeffs = jnp.einsum('pik,pkf->pif', operators.astype(jnp.float32), masked.astype(jnp.float32), precision=lax.Precision.HIGHEST).astype(jnp.bfloat16)
    points = jnp.asarray(stencil())
    inverse = 1.0 / radius
    squared = jnp.zeros((count, points.shape[0], xyz.shape[2]), jnp.float32)
    for component in range(3):
        offset = points[None, :, component, None] - xyz[:, None, component, :]
        squared = squared + offset * offset
    scaled = squared * (inverse * inverse)[:, None, None]
    kernel = scaled * jnp.sqrt(scaled)
    unit_points = points[None, :, :] * inverse[:, None, None]
    powers = [jnp.ones_like(unit_points), unit_points, unit_points * unit_points, unit_points * unit_points * unit_points]
    monomials = [powers[first][..., 0] * powers[second][..., 1] * powers[third][..., 2] for first, second, third in EXPONENTS]
    design = jnp.concatenate([kernel, jnp.stack(monomials, -1)], -1).astype(jnp.bfloat16)
    values = jnp.einsum('pmi,pif->pmf', design.astype(jnp.float32), coeffs.astype(jnp.float32), precision=lax.Precision.HIGHEST)
    distance = jnp.sqrt(lax.optimization_barrier(jnp.sum(points * points, 1)))[None, :] * inverse[:, None]
    blend = jnp.maximum(1.0 - distance, 0.0) ** 4 * (4.0 * distance + 1.0)
    terms = values * blend[:, :, None]
    return terms.reshape(count, 9, 9, 4, fields)

def reference(node_values, fit_ops, node_xyz, patch_nodes, patch_valid, patch_cell, patch_radius, cell_scale):
    fields = node_values.shape[3]
    padded = jnp.pad(node_values, ((0, 0), (1, 1), (0, 0), (0, 0)))
    tiles = TILES_X * TILES_Y

    def tile_step(grid, inputs):
        tile_id, operators, xyz, indices, valid, cells, radius = inputs
        tile_x = tile_id // TILES_Y
        tile_y = tile_id % TILES_Y
        rows = (3 * tile_x - 1 + jnp.arange(5, dtype=jnp.int32)) % (3 * TILES_X)
        window = lax.dynamic_slice_in_dim(jnp.take(padded, rows, axis=0), 3 * tile_y, 5, 1)
        flat = window.reshape(25 * window.shape[2], fields)
        gathered = jnp.take(flat, indices, axis=0)
        terms = patch_terms(gathered, operators, xyz, valid, radius)
        anchor = jnp.stack([tile_x * CX, tile_y * CY, jnp.zeros((), jnp.int32)]).astype(jnp.int32)
        zero = jnp.zeros((), jnp.int32)

        def place(index, acc):
            start = (cells[index] + anchor).astype(jnp.int32)
            corner = (start[0], start[1], start[2], zero)
            block = lax.dynamic_slice(acc, corner, terms.shape[1:])
            return lax.dynamic_update_slice(acc, block + terms[index], corner)
        return (lax.fori_loop(0, PATCH_DEV, place, grid), None)
    start_grid = jnp.zeros((NX + 8, NY + 8, CZ, fields), jnp.float32)
    inputs = (jnp.arange(tiles, dtype=jnp.int32), fit_ops.reshape((tiles,) + fit_ops.shape[2:]), node_xyz.reshape((tiles,) + node_xyz.shape[2:]), patch_nodes.reshape((tiles,) + patch_nodes.shape[2:]), patch_valid.reshape((tiles,) + patch_valid.shape[2:]), patch_cell.reshape((tiles,) + patch_cell.shape[2:]), patch_radius.reshape((tiles,) + patch_radius.shape[2:]))
    grid, unused = lax.scan(tile_step, start_grid, inputs)
    folded = grid[4:NX + 4]
    folded = folded.at[:4].add(grid[NX + 4:NX + 8])
    folded = folded.at[NX - 4:].add(grid[:4])
    folded = folded[:, 4:NY + 4]
    return (cell_scale[..., None] * folded).astype(jnp.bfloat16)
```

```python
import jax
import jax.numpy as jnp
from jax import lax
from jax.experimental import pallas as pl
from jax.experimental.pallas import tpu as pltpu
from jax.sharding import PartitionSpec as P

REACH = 4
SPAN = 2 * REACH + 1
LAYERS = 4
NEAR = 3
EXPONENTS = (
    (0, 0, 0),
    (1, 0, 0),
    (0, 1, 0),
    (0, 0, 1),
    (2, 0, 0),
    (1, 1, 0),
    (1, 0, 1),
    (0, 2, 0),
    (0, 1, 1),
    (0, 0, 2),
    (3, 0, 0),
    (2, 1, 0),
    (2, 0, 1),
    (1, 2, 0),
    (1, 1, 1),
    (1, 0, 2),
    (0, 3, 0),
    (0, 2, 1),
    (0, 1, 2),
    (0, 0, 3),
)
DISTANCES = sorted({a * a + b * b for a in range(REACH + 1) for b in range(REACH + 1)})
VMEM = pl.BlockSpec(memory_space=pltpu.VMEM)
SMEM = pl.BlockSpec(memory_space=pltpu.SMEM)


def up(value, multiple):
    return -(-value // multiple) * multiple


def swap(size, first, wrap):
    pairs = []
    for i in range(first, size, 2):
        j = i + 1
        if j == size:
            if not wrap:
                continue
            j = 0
        pairs += [(i, j), (j, i)]
    return pairs


def design_kernel(nodes, unknowns, cells_ref, radius_ref, xyz_ref, scale_ref, design_ref, wide_ref, pos, ax, by, bc, bm, bl):
    patches = design_ref.shape[0]
    lanes = design_ref.shape[2]
    depth = bl.shape[1]
    tile = (depth, lanes)
    pos[:, :, 0:nodes] = xyz_ref[...]
    lane = lax.broadcasted_iota(jnp.int32, (1, lanes), 1)
    is_node = lane < nodes
    used = lane < unknowns
    power = []
    for axis in range(3):
        rows = []
        for degree in range(1, 4):
            hit = lane < 0
            for index, triple in enumerate(EXPONENTS):
                if triple[axis] == degree:
                    hit = hit | (lane == nodes + index)
            rows.append(hit)
        power.append(rows)

    def raised(value, axis):
        one, two, three = power[axis]
        square = value * value
        out = jnp.where(one, value, 1.0)
        out = jnp.where(two, square, out)
        return jnp.where(three, square * value, out)

    across = (lax.broadcasted_iota(jnp.int32, (16, lanes), 0) - REACH).astype(jnp.float32)
    layer = lax.broadcasted_iota(jnp.int32, tile, 0)

    def patch(p, carry):
        inverse = 1.0 / jnp.full((1, lanes), radius_ref[0, p], jnp.float32)
        deep = (layer - cells_ref[p, 2]).astype(jnp.float32) - 1.5
        x = jnp.where(is_node, pos[0, pl.ds(p, 1), :], 0.0)
        y = jnp.where(is_node, pos[1, pl.ds(p, 1), :], 0.0)
        z = jnp.where(is_node, pos[2, pl.ds(p, 1), :], 0.0)
        dx = (across - x) * inverse
        dy = (across - y) * inverse
        dz = (deep - z) * inverse
        ax[...] = jnp.where(is_node, dx * dx, raised(dx, 0))
        by[...] = jnp.where(is_node, dy * dy, raised(dy, 1))
        cz = jnp.where(is_node, dz * dz, raised(dz, 2))
        for ey in range(SPAN):
            row = by[ey : ey + 1, :]
            bc[ey] = row + cz
            bm[ey] = (row * cz)[:, lanes - 128 :]
        inside = jnp.abs(deep[:, :128]) < 2.0
        near = inverse[:, :128]
        for index, flat in enumerate(DISTANCES):
            rho = jnp.sqrt(float(flat) + deep[:, :128] * deep[:, :128]) * near
            left = jnp.maximum(1.0 - rho, 0.0)
            left = left * left
            bl[index] = jnp.where(inside, left * left * (4.0 * rho + 1.0), 0.0)
        repeats = lanes // 128

        def one(spot):
            ex, ey = divmod(spot, SPAN)
            row = ax[ex : ex + 1, :]
            part = row + bc[ey]
            part = part * part * lax.rsqrt(jnp.maximum(part, 1e-30))
            last = row[:, lanes - 128 :] * bm[ey]
            low = (ex - REACH) ** 2 + (ey - REACH) ** 2
            blend = bl[DISTANCES.index(low)]
            pieces = [part[:, c * 128 : c * 128 + 128] for c in range(repeats)]
            pieces[-1] = jnp.where(is_node[:, lanes - 128 :], pieces[-1], last)
            pieces = [piece * blend for piece in pieces]
            pieces[-1] = jnp.where(used[:, lanes - 128 :], pieces[-1], 0.0)
            return jnp.concatenate(pieces, 1)

        for spot in range(0, SPAN * SPAN, 2):
            first = one(spot)
            second = one(spot + 1) if spot + 1 < SPAN * SPAN else jnp.zeros_like(first)
            pair = jnp.concatenate([first, second], 0).astype(jnp.bfloat16)
            design_ref[p, spot * depth : (spot + 2) * depth, :] = pair
        return carry

    lax.fori_loop(0, patches, patch, 0)
    for i in range(scale_ref.shape[0]):
        columns = scale_ref[i]
        for j in range(scale_ref.shape[2]):
            wide_ref[i, j] = jnp.broadcast_to(columns[:, j : j + 1], wide_ref.shape[2:])


def select_kernel(sides, subregion, tile, cells_ref, valid_ref, nodes_ref, fit_ref, out_ref, hot):
    patches, slots = nodes_ref.shape
    lane = lax.broadcasted_iota(jnp.int32, (1, slots), 1)
    node = lax.broadcasted_iota(jnp.int32, (subregion, slots), 0)
    for p in range(patches):
        index = nodes_ref[p : p + 1, :]
        where = lax.div(index, jnp.int32(subregion))
        inner = index - where * subregion
        a = jnp.zeros_like(where)
        for t in range(1, sides[0] + 2):
            a = a + jnp.where(where >= t * (sides[1] + 2), 1, 0)
        b = where - a * (sides[1] + 2)
        home_x = (cells_ref[p, 0] * sides[0]) // tile[0]
        home_y = (cells_ref[p, 1] * sides[1]) // tile[1]
        local = (a - home_x) * NEAR + (b - home_y)
        local = jnp.where(lane < valid_ref[0, p], local, -1)
        for s in range(NEAR * NEAR):
            row = jnp.where(local == s, inner, -1)
            hot[s * subregion : (s + 1) * subregion, :] = jnp.where(node == row, 1.0, 0.0).astype(jnp.bfloat16)
        out_ref[p] = lax.dot_general(
            fit_ref[p], hot[...], (((1,), (1,)), ((), ())), preferred_element_type=jnp.float32
        ).astype(jnp.bfloat16)


def blend_kernel(
    tile, cells_ref, turn_ref, own_ref, a_ref, b_ref, c_ref, d_ref, e_ref, f_ref, select_ref, design_ref,
    inner_ref, xa_ref, xb_ref, ca_ref, cb_ref, za_ref, zb_ref, near, acc,
):
    sx, sy, subregion, fields = own_ref.shape
    patches, unknowns, _ = select_ref.shape
    cx, cy = tile
    depth = acc.shape[2]
    rows = SPAN * SPAN * depth
    odd_x, odd_y = turn_ref[0], turn_ref[1]
    xa = (1 - odd_x) * (sx + 1)
    xb = odd_x * (sx + 1)
    ya = (1 - odd_y) * (sy + 1)
    yb = odd_y * (sy + 1)
    near[1 : sx + 1, 1 : sy + 1] = own_ref[...]
    near[xa, 1 : sy + 1] = a_ref[...]
    near[xb, 1 : sy + 1] = b_ref[...]
    near[1 : sx + 1, ya] = c_ref[...]
    near[1 : sx + 1, yb] = d_ref[...]
    near[xa, ya] = e_ref[0]
    near[xa, yb] = e_ref[1]
    near[xb, ya] = f_ref[0]
    near[xb, yb] = f_ref[1]
    acc[...] = jnp.zeros_like(acc)
    for p in range(patches):
        first, second = cells_ref[p, 0], cells_ref[p, 1]
        home_x = (first * sx) // cx
        home_y = (second * sy) // cy
        window = jnp.concatenate(
            [near[home_x + r, pl.ds(home_y, NEAR)].reshape(NEAR * subregion, fields) for r in range(NEAR)], 0
        )
        coeffs = jnp.dot(select_ref[p], window, preferred_element_type=jnp.float32).astype(jnp.bfloat16)
        values = jnp.dot(design_ref[p, :rows, :unknowns], coeffs, preferred_element_type=jnp.float32)
        values = values.reshape(SPAN, SPAN, depth, fields)
        for ex in range(SPAN):
            spot = (first + ex, pl.ds(second, SPAN))
            acc[spot] = acc[spot] + values[ex]
    ra = (1 - odd_x) * (cx + REACH)
    rb = odd_x * (cx + REACH)
    sa = (1 - odd_y) * (cy + REACH)
    sb = odd_y * (cy + REACH)
    rim, in_x, in_y = REACH, pl.ds(REACH, cx), pl.ds(REACH, cy)
    for ref, r in ((ca_ref, ra), (cb_ref, rb)):
        for index, s in ((0, sa), (1, sb)):
            ref[index] = acc[pl.ds(r, rim), pl.ds(s, rim)].astype(ref.dtype)
    for ref, r in ((xa_ref, ra), (xb_ref, rb)):
        ref[...] = acc[pl.ds(r, rim), in_y].astype(ref.dtype)
    for ref, s in ((za_ref, sa), (zb_ref, sb)):
        ref[...] = acc[in_x, pl.ds(s, rim)]
    inner_ref[...] = acc[in_x, in_y]


def relay_kernel(turn_ref, za_ref, zb_ref, ca_ref, cb_ref, outa_ref, outb_ref):
    odd = turn_ref[0]
    last = za_ref.shape[0] - REACH
    at = ((1 - odd) * last, odd * last)
    for index, (z_ref, out_ref) in enumerate(((za_ref, outa_ref), (zb_ref, outb_ref))):
        out_ref[...] = z_ref[...].astype(out_ref.dtype)
        for c_ref, r in ((ca_ref, at[0]), (cb_ref, at[1])):
            rows = pl.ds(r, REACH)
            out_ref[rows] = (z_ref[rows] + c_ref[index].astype(jnp.float32)).astype(out_ref.dtype)


def finish_kernel(turn_ref, inner_ref, wide_ref, xa_ref, xb_ref, za_ref, zb_ref, out_ref, acc):
    cx, cy, depth, fields = inner_ref.shape
    odd_x, odd_y = turn_ref[0], turn_ref[1]
    acc[...] = inner_ref[...]
    for ref, r in ((xa_ref, (1 - odd_x) * (cx - REACH)), (xb_ref, odd_x * (cx - REACH))):
        rows = pl.ds(r, REACH)
        acc[rows] = acc[rows] + ref[...].astype(jnp.float32)
    for ref, s in ((za_ref, (1 - odd_y) * (cy - REACH)), (zb_ref, odd_y * (cy - REACH))):
        rows = pl.ds(s, REACH)
        acc[:, rows] = acc[:, rows] + ref[...].astype(jnp.float32)
    for f in range(0, fields, 128):
        out_ref[:, :, :, f : f + 128] = (acc[:, :, :, f : f + 128] * wide_ref[...]).astype(out_ref.dtype)


def params(megabytes):
    return pltpu.CompilerParams(vmem_limit_bytes=megabytes * 2**20)


def local(node_values, fit_ops, node_xyz, patch_nodes, patch_valid, patch_cell, patch_radius, cell_scale):
    sx, sy, subregion, fields = node_values.shape
    patches, unknowns, slots = fit_ops.shape[2:]
    cx, cy, depth = cell_scale.shape
    across, along = lax.axis_size("gx"), lax.axis_size("gy")
    kind = node_values.dtype
    full = jnp.float32
    shape = jax.ShapeDtypeStruct
    lanes = up(unknowns, 128)
    rows = up(SPAN * SPAN, 2) * depth

    def send(block, axis, first):
        size = across if axis == "gx" else along
        return lax.ppermute(block, axis, swap(size, first, axis == "gx"))

    odd_x = lax.axis_index("gx") % 2
    odd_y = lax.axis_index("gy") % 2
    turn = jnp.stack([odd_x, odd_y]).astype(jnp.int32)
    cells = patch_cell[0, 0]

    far_x, far_y = (1 - odd_x) * (sx - 1), (1 - odd_y) * (sy - 1)
    back_x, back_y = odd_x * (sx - 1), odd_y * (sy - 1)
    column = lambda j: lax.dynamic_index_in_dim(node_values, j, 1, keepdims=False)
    line = lambda i: lax.dynamic_index_in_dim(node_values, i, 0, keepdims=False)
    from_ya = send(column(far_y), "gy", 0)
    from_yb = send(column(back_y), "gy", 1)
    from_xb = send(line(back_x), "gx", 1)
    from_xa = send(line(far_x), "gx", 0)
    pick = lambda block, i: lax.dynamic_index_in_dim(block, i, 0, keepdims=False)
    corner_b = send(jnp.stack([pick(from_ya, back_x), pick(from_yb, back_x)]), "gx", 1)
    corner_a = send(jnp.stack([pick(from_ya, far_x), pick(from_yb, far_x)]), "gx", 0)

    design, wide = pl.pallas_call(
        lambda *refs: design_kernel(slots, unknowns, *refs),
        out_shape=(shape((patches, rows, lanes), kind), shape((cx, cy, depth, 128), full)),
        in_specs=[SMEM, SMEM, VMEM, VMEM],
        out_specs=(VMEM, VMEM),
        scratch_shapes=[
            pltpu.VMEM((3, patches, lanes), full),
            pltpu.VMEM((16, lanes), full),
            pltpu.VMEM((16, lanes), full),
            pltpu.VMEM((SPAN, depth, lanes), full),
            pltpu.VMEM((SPAN, depth, 128), full),
            pltpu.VMEM((len(DISTANCES), depth, 128), full),
        ],
        compiler_params=params(16),
        cost_estimate=pl.CostEstimate(flops=40_000_000, bytes_accessed=6_000_000, transcendentals=2_000_000),
        name="design",
    )(cells, patch_radius[0], node_xyz[0, 0].transpose(1, 0, 2), cell_scale.transpose(0, 2, 1))

    select = pl.pallas_call(
        lambda *refs: select_kernel((sx, sy), subregion, (cx, cy), *refs),
        out_shape=shape((patches, unknowns, NEAR * NEAR * subregion), kind),
        in_specs=[SMEM, SMEM, VMEM, VMEM],
        out_specs=VMEM,
        scratch_shapes=[pltpu.VMEM((NEAR * NEAR * subregion, slots), kind)],
        compiler_params=params(20),
        cost_estimate=pl.CostEstimate(flops=1_800_000_000, bytes_accessed=8_000_000, transcendentals=0),
        name="select",
    )(cells, patch_valid[0], patch_nodes[0, 0], fit_ops[0, 0])

    block = lambda *dims, kind=kind: shape(dims + (depth, fields), kind)
    inner, xa, xb, ca, cb, za, zb = pl.pallas_call(
        lambda *refs: blend_kernel((cx, cy), *refs),
        out_shape=(
            block(cx, cy, kind=full),
            block(REACH, cy),
            block(REACH, cy),
            block(2, REACH, REACH),
            block(2, REACH, REACH),
            block(cx, REACH, kind=full),
            block(cx, REACH, kind=full),
        ),
        in_specs=[SMEM, SMEM] + [VMEM] * 9,
        out_specs=(VMEM,) * 7,
        scratch_shapes=[
            pltpu.VMEM((sx + 2, sy + 2, subregion, fields), kind),
            pltpu.VMEM((cx + 2 * REACH, cy + 2 * REACH, depth, fields), full),
        ],
        compiler_params=params(32),
        cost_estimate=pl.CostEstimate(flops=2_500_000_000, bytes_accessed=20_000_000, transcendentals=0),
        name="blend",
    )(cells, turn, node_values, from_xa, from_xb, from_ya, from_yb, corner_a, corner_b, select, design)

    got_cb = send(cb, "gx", 1)
    got_ca = send(ca, "gx", 0)
    got_xb = send(xb, "gx", 1)
    got_xa = send(xa, "gx", 0)
    za, zb = pl.pallas_call(
        relay_kernel,
        out_shape=(block(cx, REACH), block(cx, REACH)),
        in_specs=[SMEM] + [VMEM] * 4,
        out_specs=(VMEM, VMEM),
        compiler_params=params(8),
        cost_estimate=pl.CostEstimate(flops=400_000, bytes_accessed=1_500_000, transcendentals=0),
        name="relay",
    )(turn, za, zb, got_ca, got_cb)
    got_za = send(za, "gy", 0)
    got_zb = send(zb, "gy", 1)
    return pl.pallas_call(
        finish_kernel,
        out_shape=block(cx, cy),
        in_specs=[SMEM] + [VMEM] * 6,
        out_specs=VMEM,
        scratch_shapes=[pltpu.VMEM((cx, cy, depth, fields), full)],
        compiler_params=params(12),
        cost_estimate=pl.CostEstimate(flops=2_000_000, bytes_accessed=4_000_000, transcendentals=0),
        name="finish",
    )(turn, inner, wide, got_xa, got_xb, got_za, got_zb)


def solution(mesh):
    placed = (
        P("gx", "gy", None, None),
        P("gx", "gy", None, None, None),
        P("gx", "gy", None, None, None),
        P("gx", "gy", None, None),
        P("gx", "gy", None),
        P("gx", "gy", None, None),
        P("gx", "gy", None),
        P("gx", "gy", None),
    )
    return jax.shard_map(
        local, mesh=mesh, in_specs=placed, out_specs=P("gx", "gy", None, None), check_vma=False
    )
```

```python
import jax
import jax.numpy as jnp
from jax import lax
from jax.experimental import pallas as pl
from jax.experimental.pallas import tpu as pltpu
from jax.sharding import PartitionSpec as P

REACH = 4
SPAN = 2 * REACH + 1
LAYERS = 4
NEAR = 3
EXPONENTS = (
    (0, 0, 0),
    (1, 0, 0),
    (0, 1, 0),
    (0, 0, 1),
    (2, 0, 0),
    (1, 1, 0),
    (1, 0, 1),
    (0, 2, 0),
    (0, 1, 1),
    (0, 0, 2),
    (3, 0, 0),
    (2, 1, 0),
    (2, 0, 1),
    (1, 2, 0),
    (1, 1, 1),
    (1, 0, 2),
    (0, 3, 0),
    (0, 2, 1),
    (0, 1, 2),
    (0, 0, 3),
)
DISTANCES = sorted({a * a + b * b for a in range(REACH + 1) for b in range(REACH + 1)})
SPOTS = [(ex, ey) for ex in range(SPAN) for ey in range(SPAN - 1)] + [(ex, SPAN - 1) for ex in range(SPAN)]
VMEM = pl.BlockSpec(memory_space=pltpu.VMEM)
SMEM = pl.BlockSpec(memory_space=pltpu.SMEM)


SMALL = pl.CostEstimate(flops=1000, bytes_accessed=1000, transcendentals=0)
LARGE = pl.CostEstimate(flops=4_000_000_000, bytes_accessed=40_000_000, transcendentals=0)


def up(value, multiple):
    return -(-value // multiple) * multiple


def parity():
    return lax.rem(lax.axis_index("gx"), 2), lax.rem(lax.axis_index("gy"), 2)


def swap(size, first, wrap):
    pairs = []
    for i in range(first, size, 2):
        j = i + 1
        if j == size:
            if not wrap:
                continue
            j = 0
        pairs += [(i, j), (j, i)]
    return pairs


def pack_kernel(count, nodes_ref, *refs):
    plain, sent, copied, sems = refs[:count], refs[count : count + 6], refs[count + 6 : -1], refs[-1]
    ya_ref, yb_ref, xa_ref, xb_ref, da_ref, db_ref = sent
    sx, sy = nodes_ref.shape[:2]
    odd_x, odd_y = parity()
    far_x, back_x = (1 - odd_x) * (sx - 1), odd_x * (sx - 1)
    far_y, back_y = (1 - odd_y) * (sy - 1), odd_y * (sy - 1)
    pairs = (
        (nodes_ref.at[back_x, back_y], db_ref),
        (nodes_ref.at[back_x, far_y], da_ref),
        (nodes_ref.at[:, far_y], ya_ref),
        (nodes_ref.at[:, back_y], yb_ref),
        (nodes_ref.at[back_x], xb_ref),
        (nodes_ref.at[far_x], xa_ref),
        *zip(plain, copied),
    )
    copies = [pltpu.make_async_copy(source, target, sems.at[index]) for index, (source, target) in enumerate(pairs)]
    for copy in copies:
        copy.start()
    for copy in copies:
        copy.wait()


def extend_kernel(ya_ref, yb_ref, own_ref, out_ref):
    odd_x, odd_y = parity()
    far_x = (1 - odd_x) * (ya_ref.shape[0] - 1)
    last = out_ref.shape[0] - 1
    out_ref[1:last] = own_ref[...]
    out_ref[(1 - odd_y) * last] = ya_ref[far_x]
    out_ref[odd_y * last] = yb_ref[far_x]


def prepare_kernel(
    sides, subregion, tile, radius_ref, xyz_ref, scale_ref, cells_ref, valid_ref, nodes_ref, far_ref,
    design_ref, wide_ref, hot_ref, fit_ref, near_ref, split, places, sem, *scratch,
):
    copy = pltpu.make_async_copy(far_ref, near_ref, sem)
    copy.start()
    design_kernel(nodes_ref.shape[1], near_ref.shape[2], radius_ref, xyz_ref, scale_ref, design_ref, wide_ref, *scratch)
    copy.wait()
    choose(sides, subregion, tile, cells_ref, valid_ref, nodes_ref, near_ref, hot_ref, fit_ref, split, places)


def design_kernel(nodes, unknowns, radius_ref, xyz_ref, scale_ref, design_ref, wide_ref, pos, ax, by, ax2, bc, bm, bl):
    patches = design_ref.shape[0]
    lanes = design_ref.shape[2]
    tile = (2 * LAYERS, lanes)
    pos[:, :, 0:nodes] = xyz_ref[...]
    lane = lax.broadcasted_iota(jnp.int32, (1, lanes), 1)
    is_node = lane < nodes
    used = lane < unknowns
    power = []
    for axis in range(3):
        rows = []
        for degree in range(1, 4):
            hit = lane < 0
            for index, triple in enumerate(EXPONENTS):
                if triple[axis] == degree:
                    hit = hit | (lane == nodes + index)
            rows.append(hit)
        power.append(rows)

    def raised(value, axis):
        one, two, three = power[axis]
        square = value * value
        out = jnp.where(one, value, jnp.where(used, 1.0, 0.0))
        out = jnp.where(two, square, out)
        return jnp.where(three, square * value, out)

    across = (lax.broadcasted_iota(jnp.int32, (16, lanes), 0) - REACH).astype(jnp.float32)
    layer = lax.broadcasted_iota(jnp.int32, tile, 0)
    upper = layer < LAYERS
    deep = jnp.where(upper, layer, layer - LAYERS).astype(jnp.float32) - 0.5 * (LAYERS - 1)
    tail = slice(lanes - 128, lanes)
    half = SPAN // 2

    def patch(p, carry):
        inverse = 1.0 / jnp.full((1, lanes), radius_ref[0, p], jnp.float32)
        x = jnp.where(is_node, pos[0, pl.ds(p, 1), :], 0.0)
        y = jnp.where(is_node, pos[1, pl.ds(p, 1), :], 0.0)
        z = jnp.where(is_node, pos[2, pl.ds(p, 1), :], 0.0)
        dx = (across - x) * inverse
        dy = (across - y) * inverse
        dz = (deep - z) * inverse
        ax[...] = jnp.where(is_node, dx * dx, raised(dx, 0))
        by[...] = jnp.where(is_node, dy * dy, raised(dy, 1))
        cz = jnp.where(is_node, dz * dz + 1e-30, raised(dz, 2))
        for i in range(half + 1):
            low, high = 2 * i, min(2 * i + 1, SPAN - 1)
            row = jnp.where(upper, by[low : low + 1, :], by[high : high + 1, :])
            bc[i] = row + cz
            bm[i] = row[:, tail] * cz[:, tail]
            ax2[i] = jnp.where(upper, ax[low : low + 1, :], ax[high : high + 1, :])
        for index, flat in enumerate(DISTANCES):
            rho = jnp.sqrt(float(flat) + deep[:, :128] * deep[:, :128]) * inverse[:, :128]
            left = jnp.maximum(1.0 - rho, 0.0)
            left = left * left
            bl[index] = left * left * (4.0 * rho + 1.0)

        def pair(spots):
            (ex, ey), (fx, fy) = spots[0], spots[-1]
            row = ax[ex : ex + 1, :] if ex == fx else ax2[ex // 2]
            part = row + bc[ey // 2]
            part = part * part * lax.rsqrt(part)
            last = row[:, tail] * bm[ey // 2]
            blend = [bl[DISTANCES.index((i - REACH) ** 2 + (j - REACH) ** 2)] for i, j in ((ex, ey), (fx, fy))]
            blend = blend[0] if (ex, ey) == (fx, fy) else jnp.where(upper[:, :128], blend[0], blend[1])
            if len(spots) == 1:
                blend = jnp.where(upper[:, :128], blend, 0.0)
            pieces = [part[:, c : c + 128] for c in range(0, lanes, 128)]
            pieces[-1] = jnp.where(is_node[:, tail], pieces[-1], last)
            return jnp.concatenate([piece * blend for piece in pieces], 1)

        for spot in range(0, len(SPOTS), 4):
            rows = [pair(SPOTS[q : q + 2]) if q < len(SPOTS) else jnp.zeros(tile, jnp.float32) for q in (spot, spot + 2)]
            design_ref[p, spot * LAYERS : (spot + 4) * LAYERS, :] = jnp.concatenate(rows, 0).astype(jnp.bfloat16)
        return carry

    lax.fori_loop(0, patches, patch, 0)
    for i in range(scale_ref.shape[0]):
        columns = scale_ref[i]
        for j in range(scale_ref.shape[2]):
            wide_ref[i, j] = jnp.broadcast_to(columns[:, j : j + 1], wide_ref.shape[2:])


def choose(sides, subregion, tile, cells_ref, valid_ref, nodes_ref, fit_ref, hot, fit, wide, places):
    patches, slots = nodes_ref.shape
    unknowns = fit.shape[1]
    padded = hot.shape[1]
    kind = fit.dtype
    lane = lax.broadcasted_iota(jnp.int32, (1, slots), 1)
    places[...] = jnp.full(places.shape, -1.0, jnp.float32)
    for c in range(0, unknowns, 128):
        width = min(128, unknowns - c)
        wide[c // 128, :, :width] = fit_ref[:, :, c : c + width].astype(jnp.float32).reshape(slots * patches, width)
    for p in range(patches):
        index = nodes_ref[p : p + 1, :]
        where = lax.div(index, jnp.int32(subregion))
        a = jnp.zeros_like(where)
        for t in range(1, sides[0] + 2):
            a = a + jnp.where(where >= t * (sides[1] + 2), 1, 0)
        b = where - a * (sides[1] + 2)
        home_x, home_y = home(sides, tile, cells_ref, p)
        local = (a - home_x) * NEAR + (b - home_y)
        local = jnp.where(lane < valid_ref[0, p], local, -1)
        places[0, p : p + 1, 0:slots] = (index - where * subregion).astype(jnp.float32)
        places[1, p : p + 1, 0:slots] = local.astype(jnp.float32)
    inner, local = places[0].T, places[1].T
    node = lax.broadcasted_iota(jnp.int32, (padded, subregion), 1).astype(jnp.float32).astype(kind)
    one, zero = jnp.ones((), kind), jnp.zeros((), kind)
    fit[:, :, slots:] = jnp.zeros((patches, unknowns, padded - slots), kind)
    for p in range(patches):
        column = jnp.broadcast_to(inner[:padded, p : p + 1], (padded, subregion)).astype(kind)
        one_hot = jnp.where(node == column, one, zero)
        column = jnp.broadcast_to(local[:padded, p : p + 1], (padded, subregion)).astype(kind)
        for s in range(NEAR * NEAR):
            hot[p, :, s * subregion : (s + 1) * subregion] = jnp.where(column == jnp.full((), s, kind), one_hot, zero)
        for c in range(0, unknowns, 128):
            width = min(128, unknowns - c)
            piece = wide[c // 128, pl.ds(p, slots, stride=patches), :]
            fit[p, c : c + width, 0:slots] = piece.T[:width].astype(kind)


def home(sides, tile, cells_ref, p):
    return (cells_ref[0, 0, p] * sides[0]) // tile[0], (cells_ref[1, 0, p] * sides[1]) // tile[1]


def sample_kernel(
    tile, cells_ref, own_ref, b_ref, c_ref, d_ref, e_ref, f_ref, hot_ref, out_ref, near,
):
    sx, sy, subregion, fields = own_ref.shape
    odd_x, odd_y = parity()
    xa = (1 - odd_x) * (sx + 1)
    xb = odd_x * (sx + 1)
    ya = (1 - odd_y) * (sy + 1)
    yb = odd_y * (sy + 1)
    near[1 : sx + 1, 1 : sy + 1] = own_ref[...]
    near[xb, 1 : sy + 1] = b_ref[...]
    near[1 : sx + 1, ya] = c_ref[...]
    near[1 : sx + 1, yb] = d_ref[...]
    near[xb, ya] = e_ref[...]
    near[xb, yb] = f_ref[...]
    near[xa] = jnp.zeros(near.shape[1:], near.dtype)
    for p in range(hot_ref.shape[0]):
        home_x, home_y = home((sx, sy), tile, cells_ref, p)
        window = jnp.concatenate(
            [near[home_x + r, pl.ds(home_y, NEAR)].reshape(NEAR * subregion, fields) for r in range(NEAR)], 0
        )
        out_ref[p] = jnp.dot(hot_ref[p], window, preferred_element_type=jnp.float32)


def blend_kernel(
    sides, tile, cells_ref, side_ref, sample_ref, hot_ref, fit_ref, design_ref,
    inner_ref, xa_ref, xb_ref, da_ref, db_ref, za_ref, zb_ref, chosen, coeffs, values, acc,
):
    sx, sy = sides
    subregion, fields = side_ref.shape[1:]
    patches, unknowns, _ = fit_ref.shape
    cx, cy = tile
    rows = len(SPOTS) * LAYERS
    odd_x, odd_y = parity()
    xa = (1 - odd_x) * (sx + 1)
    acc[...] = jnp.zeros_like(acc)
    for p in range(patches):
        home_x, home_y = home(sides, tile, cells_ref, p)
        row = xa - home_x
        here = (row >= 0) & (row < NEAR)
        spot = pl.multiple_of(jnp.where(here, row, 0) * (NEAR * subregion), NEAR * subregion)
        side = side_ref[pl.ds(home_y, NEAR)].reshape(NEAR * subregion, fields)
        side = side * jnp.where(here, 1.0, 0.0).astype(side.dtype)
        extra = jnp.dot(hot_ref[p, :, pl.ds(spot, NEAR * subregion)], side, preferred_element_type=jnp.float32)
        chosen[p] = (sample_ref[p] + extra).astype(chosen.dtype)
    for p in range(patches):
        coeffs[p] = jnp.dot(fit_ref[p], chosen[p], preferred_element_type=jnp.float32).astype(coeffs.dtype)

    def place(p):
        first, second, third = cells_ref[0, 0, p], cells_ref[1, 0, p], cells_ref[2, 0, p]
        for s, (ex, ey) in enumerate(SPOTS):
            for l in range(acc.shape[0]):
                spot = (l, first + ex, second + ey, pl.ds(third, LAYERS))
                acc[spot] = acc[spot] + values[p, s * LAYERS : (s + 1) * LAYERS, l * 128 : (l + 1) * 128]

    for p in range(patches):
        values[p] = jnp.dot(design_ref[p, :rows, :unknowns], coeffs[p], preferred_element_type=jnp.float32)
        if p:
            place(p - 1)
    place(patches - 1)

    ra = (1 - odd_x) * (cx + REACH)
    rb = odd_x * (cx + REACH)
    sa = (1 - odd_y) * (cy + REACH)
    sb = odd_y * (cy + REACH)
    rim, in_x, in_y = REACH, pl.ds(REACH, cx), pl.ds(REACH, cy)
    for l in range(acc.shape[0]):
        f = pl.ds(l * 128, 128)
        xa_ref[:, :, :, f] = acc[l, pl.ds(ra, rim)].astype(xa_ref.dtype)
        xb_ref[:, :, :, f] = acc[l, pl.ds(rb, rim), in_y].astype(xb_ref.dtype)
        for ref, s in ((da_ref, sa), (db_ref, sb)):
            ref[:, :, :, f] = acc[l, pl.ds(rb, rim), pl.ds(s, rim)].astype(ref.dtype)
        for ref, s in ((za_ref, sa), (zb_ref, sb)):
            ref[:, :, :, f] = acc[l, in_x, pl.ds(s, rim)]
        inner_ref[:, :, :, f] = acc[l, in_x, in_y]


def relay_kernel(za_ref, zb_ref, xa_ref, outa_ref, outb_ref):
    odd_x, odd_y = parity()
    cx = za_ref.shape[0]
    rows = pl.ds((1 - odd_x) * (cx - REACH), REACH)
    last = xa_ref.shape[1] - REACH
    for z_ref, out_ref, s in ((za_ref, outa_ref, (1 - odd_y) * last), (zb_ref, outb_ref, odd_y * last)):
        out_ref[...] = z_ref[...].astype(out_ref.dtype)
        got = xa_ref[:, pl.ds(s, REACH)].astype(jnp.float32)
        out_ref[rows] = (z_ref[rows] + got).astype(out_ref.dtype)


def gather_kernel(inner_ref, wide_ref, xa_ref, xb_ref, za_ref, zb_ref, out_ref):
    cx, cy, depth, fields = inner_ref.shape
    odd_x, odd_y = parity()
    far, back = pl.ds((1 - odd_x) * (cx - REACH), REACH), pl.ds(odd_x * (cx - REACH), REACH)
    for f in range(0, fields, 128):
        part = slice(f, f + 128)
        out_ref[:, :, :, part] = inner_ref[:, :, :, part] * wide_ref[...]
        got = xa_ref[:, REACH : REACH + cy, :, part].astype(jnp.float32)
        out_ref[far, :, :, part] = out_ref[far, :, :, part] + got * wide_ref[far]
        got = xb_ref[:, :, :, part].astype(jnp.float32)
        out_ref[back, :, :, part] = out_ref[back, :, :, part] + got * wide_ref[back]
        for z_ref, s in ((za_ref, (1 - odd_y) * (cy - REACH)), (zb_ref, odd_y * (cy - REACH))):
            spot = (slice(None), pl.ds(s, REACH))
            got = z_ref[:, :, :, part].astype(jnp.float32)
            out_ref[spot + (slice(None), part)] = out_ref[spot + (slice(None), part)] + got * wide_ref[spot]


def finish_kernel(base_ref, wide_ref, da_ref, db_ref, out_ref):
    cx, cy, depth, fields = base_ref.shape
    odd_x, odd_y = parity()
    back = pl.ds(odd_x * (cx - REACH), REACH)
    for f in range(0, fields, 128):
        part = slice(f, f + 128)
        out_ref[:, :, :, part] = base_ref[:, :, :, part].astype(out_ref.dtype)
        for d_ref, s in ((da_ref, (1 - odd_y) * (cy - REACH)), (db_ref, odd_y * (cy - REACH))):
            spot = (back, pl.ds(s, REACH))
            got = d_ref[:, :, :, part].astype(jnp.float32) * wide_ref[spot]
            out_ref[spot + (slice(None), part)] = (base_ref[spot + (slice(None), part)] + got).astype(out_ref.dtype)


def params(megabytes):
    return pltpu.CompilerParams(vmem_limit_bytes=megabytes * 2**20)


def local(node_values, fit_ops, node_xyz, patch_nodes, patch_valid, patch_cell, patch_radius, cell_scale):
    sx, sy, subregion, fields = node_values.shape
    patches, unknowns, slots = fit_ops.shape[2:]
    cx, cy, depth = cell_scale.shape
    across, along = lax.axis_size("gx"), lax.axis_size("gy")
    kind = node_values.dtype
    full = jnp.float32
    shape = jax.ShapeDtypeStruct
    lanes = up(unknowns, 128)
    rows = up(len(SPOTS), 4) * LAYERS
    halves = fields // 128

    pairs_x = [swap(across, first, True) for first in (0, 1)]
    pairs_y = [swap(along, first, False) for first in (0, 1)]

    def send_x(block, turn):
        return lax.ppermute(block, "gx", pairs_x[turn])

    def send_y(block, turn):
        return lax.ppermute(block, "gy", pairs_y[turn])

    def send_across(block, turn):
        both = [(a * along + c, b * along + d) for a, b in pairs_x[1] for c, d in pairs_y[turn]]
        return lax.ppermute(block, ("gx", "gy"), both)

    line = lambda *sides: shape(sides + (subregion, fields), kind)
    plain = (
        patch_cell.transpose(0, 3, 1, 2)[0],
        patch_valid[0],
        patch_nodes[0, 0],
        patch_radius[0],
        node_xyz[0, 0].transpose(1, 0, 2),
        cell_scale.transpose(0, 2, 1),
    )
    packed = pl.pallas_call(
        lambda *refs: pack_kernel(len(plain), *refs),
        out_shape=(line(sx), line(sx), line(sy), line(sy), line(), line()) + tuple(shape(x.shape, x.dtype) for x in plain),
        in_specs=[pl.BlockSpec(memory_space=pl.ANY)] * (1 + len(plain)),
        out_specs=(VMEM,) * (6 + len(plain)),
        scratch_shapes=[pltpu.SemaphoreType.DMA((6 + len(plain),))],
        compiler_params=params(4),
        cost_estimate=SMALL,
        name="pack",
    )(*[pltpu.with_memory_space_constraint(x, pltpu.HBM) for x in (node_values, *plain)])
    to_ya, to_yb, to_xa, to_xb, to_da, to_db, cells, valid, indices, radius, xyz, scale = packed
    from_ya = send_y(to_ya, 0)
    from_yb = send_y(to_yb, 1)
    from_xb = send_x(to_xb, 1)
    from_da = send_across(to_da, 0)
    from_db = send_across(to_db, 1)
    window = NEAR * NEAR * subregion
    padded = up(slots, 16)
    far = pltpu.with_memory_space_constraint(fit_ops[0, 0].transpose(2, 0, 1), pltpu.HBM)
    design, wide, hot, fit = pl.pallas_call(
        lambda *refs: prepare_kernel((sx, sy), subregion, (cx, cy), *refs),
        out_shape=(
            shape((patches, rows, lanes), kind),
            shape((cx, cy, depth, 128), full),
            shape((patches, padded, window), kind),
            shape((patches, unknowns, padded), kind),
        ),
        in_specs=[SMEM, VMEM, VMEM, SMEM, SMEM, VMEM, pl.BlockSpec(memory_space=pl.ANY)],
        out_specs=(VMEM,) * 4,
        scratch_shapes=[
            pltpu.VMEM(far.shape, kind),
            pltpu.VMEM((lanes // 128, slots * patches, 128), full),
            pltpu.VMEM((2, patches, up(padded, 128)), full),
            pltpu.SemaphoreType.DMA,
            pltpu.VMEM((3, patches, lanes), full),
            pltpu.VMEM((16, lanes), full),
            pltpu.VMEM((16, lanes), full),
            pltpu.VMEM((SPAN // 2 + 1, 2 * LAYERS, lanes), full),
            pltpu.VMEM((SPAN // 2 + 1, 2 * LAYERS, lanes), full),
            pltpu.VMEM((SPAN // 2 + 1, 2 * LAYERS, 128), full),
            pltpu.VMEM((len(DISTANCES), 2 * LAYERS, 128), full),
        ],
        compiler_params=params(24),
        cost_estimate=SMALL,
        name="prepare",
    )(radius, xyz, scale, cells, valid, indices, far)
    from_yb, from_ya, from_xb, from_db, from_da, hot = lax.optimization_barrier(
        (from_yb, from_ya, from_xb, from_db, from_da, hot)
    )
    to_xa = pl.pallas_call(
        extend_kernel,
        out_shape=line(sy + 2),
        in_specs=[VMEM] * 3,
        out_specs=VMEM,
        compiler_params=params(4),
        cost_estimate=SMALL,
        name="extend",
    )(from_ya, from_yb, to_xa)
    from_xa = send_x(to_xa, 0)
    samples = pl.pallas_call(
        lambda *refs: sample_kernel((cx, cy), *refs),
        out_shape=shape((patches, padded, fields), full),
        in_specs=[SMEM] + [VMEM] * 7,
        out_specs=VMEM,
        scratch_shapes=[pltpu.VMEM((sx + 2, sy + 2, subregion, fields), kind)],
        compiler_params=params(16),
        cost_estimate=LARGE,
        name="sample",
    )(cells, node_values, from_xb, from_ya, from_yb, from_da, from_db, hot)

    block = lambda *dims, kind=kind: shape(dims + (depth, fields), kind)
    inner, xa, xb, da, db, za, zb = pl.pallas_call(
        lambda *refs: blend_kernel((sx, sy), (cx, cy), *refs),
        out_shape=(
            block(cx, cy, kind=full),
            block(REACH, cy + 2 * REACH),
            block(REACH, cy),
            block(REACH, REACH),
            block(REACH, REACH),
            block(cx, REACH, kind=full),
            block(cx, REACH, kind=full),
        ),
        in_specs=[SMEM] + [VMEM] * 5,
        out_specs=(VMEM,) * 7,
        scratch_shapes=[
            pltpu.VMEM((patches, padded, fields), kind),
            pltpu.VMEM((patches, unknowns, fields), kind),
            pltpu.VMEM((patches, len(SPOTS) * LAYERS, fields), full),
            pltpu.VMEM((halves, cx + 2 * REACH, cy + 2 * REACH, depth, 128), full),
        ],
        compiler_params=params(32),
        cost_estimate=SMALL,
        name="blend",
    )(cells, from_xa, samples, hot, fit, design)

    got_xa = send_x(xa, 0)
    got_xb = send_x(xb, 1)
    got_db = send_across(db, 1)
    got_da = send_across(da, 0)
    za, zb = pl.pallas_call(
        relay_kernel,
        out_shape=(block(cx, REACH), block(cx, REACH)),
        in_specs=[VMEM] * 3,
        out_specs=(VMEM, VMEM),
        compiler_params=params(8),
        cost_estimate=SMALL,
        name="relay",
    )(za, zb, got_xa)
    got_za = send_y(za, 0)
    got_zb = send_y(zb, 1)
    base = pl.pallas_call(
        gather_kernel,
        out_shape=block(cx, cy, kind=full),
        in_specs=[VMEM] * 6,
        out_specs=VMEM,
        compiler_params=params(12),
        cost_estimate=LARGE,
        name="gather",
    )(inner, wide, got_xa, got_xb, got_za, got_zb)
    return pl.pallas_call(
        finish_kernel,
        out_shape=block(cx, cy),
        in_specs=[VMEM] * 4,
        out_specs=VMEM,
        compiler_params=params(12),
        cost_estimate=SMALL,
        name="finish",
    )(base, wide, got_da, got_db)


def solution(mesh):
    placed = (
        P("gx", "gy", None, None),
        P("gx", "gy", None, None, None),
        P("gx", "gy", None, None, None),
        P("gx", "gy", None, None),
        P("gx", "gy", None),
        P("gx", "gy", None, None),
        P("gx", "gy", None),
        P("gx", "gy", None),
    )
    return jax.shard_map(
        local, mesh=mesh, in_specs=placed, out_specs=P("gx", "gy", None, None), check_vma=False
    )
```

```python
import jax
import jax.numpy as jnp
from jax import lax
from jax.experimental import pallas as pl
from jax.experimental.pallas import tpu as pltpu
from jax.sharding import PartitionSpec as P

REACH = 4
SPAN = 2 * REACH + 1
LAYERS = 4
NEAR = 3
LOOKS = 2
EXPONENTS = (
    (0, 0, 0),
    (1, 0, 0),
    (0, 1, 0),
    (0, 0, 1),
    (2, 0, 0),
    (1, 1, 0),
    (1, 0, 1),
    (0, 2, 0),
    (0, 1, 1),
    (0, 0, 2),
    (3, 0, 0),
    (2, 1, 0),
    (2, 0, 1),
    (1, 2, 0),
    (1, 1, 1),
    (1, 0, 2),
    (0, 3, 0),
    (0, 2, 1),
    (0, 1, 2),
    (0, 0, 3),
)
DISTANCES = sorted({a * a + b * b for a in range(REACH + 1) for b in range(REACH + 1)})
SPOTS = [(ex, ey) for ex in range(SPAN) for ey in range(SPAN - 1)] + [(ex, SPAN - 1) for ex in range(SPAN)]
VMEM = pl.BlockSpec(memory_space=pltpu.VMEM)
SMEM = pl.BlockSpec(memory_space=pltpu.SMEM)


SMALL = pl.CostEstimate(flops=1000, bytes_accessed=1000, transcendentals=0)
LARGE = pl.CostEstimate(flops=4_000_000_000, bytes_accessed=40_000_000, transcendentals=0)


def up(value, multiple):
    return -(-value // multiple) * multiple


def parity():
    return lax.rem(lax.axis_index("gx"), 2), lax.rem(lax.axis_index("gy"), 2)


def partner(i, size, turn, wrap):
    j = i + 1 if i % 2 == turn else i - 1
    return j % size if wrap or 0 <= j < size else None


def routes(across, along, turn_x, turn_y):
    pairs = []
    for i in range(across):
        for j in range(along):
            to = i if turn_x is None else partner(i, across, turn_x, True)
            up_to = j if turn_y is None else partner(j, along, turn_y, False)
            if up_to is None:
                to, up_to = partner(i, across, 0, True), j
            pairs.append((i * along + j, to * along + up_to))
    return pairs


def paired(turn):
    j, odd = lax.axis_index("gy"), parity()[1]
    to = jnp.where(odd == turn, j + 1, j - 1)
    return jnp.where((to >= 0) & (to < lax.axis_size("gy")), 1.0, 0.0).astype(jnp.float32)


def pack_kernel(count, nodes_ref, *refs):
    plain, sent, copied, sems = refs[:count], refs[count : count + 6], refs[count + 6 : -1], refs[-1]
    ya_ref, yb_ref, xa_ref, xb_ref, da_ref, db_ref = sent
    sx, sy = nodes_ref.shape[:2]
    odd_x, odd_y = parity()
    far_x, back_x = (1 - odd_x) * (sx - 1), odd_x * (sx - 1)
    far_y, back_y = (1 - odd_y) * (sy - 1), odd_y * (sy - 1)
    pairs = (
        (nodes_ref.at[back_x, back_y], db_ref),
        (nodes_ref.at[back_x, far_y], da_ref),
        (nodes_ref.at[:, far_y], ya_ref),
        (nodes_ref.at[:, back_y], yb_ref),
        (nodes_ref.at[back_x], xb_ref),
        (nodes_ref.at[far_x], xa_ref),
        *zip(plain, copied),
    )
    copies = [pltpu.make_async_copy(source, target, sems.at[index]) for index, (source, target) in enumerate(pairs)]
    for copy in copies:
        copy.start()
    for copy in copies:
        copy.wait()


def extend_kernel(ya_ref, yb_ref, own_ref, out_ref):
    odd_x, odd_y = parity()
    far_x = (1 - odd_x) * (ya_ref.shape[0] - 1)
    last = out_ref.shape[0] - 1
    out_ref[1:last] = own_ref[...]
    out_ref[(1 - odd_y) * last] = ya_ref[far_x]
    out_ref[odd_y * last] = yb_ref[far_x]


def prepare_kernel(
    sides, subregion, tile, radius_ref, xyz_ref, cells_ref, valid_ref, nodes_ref, far_ref,
    design_ref, hot_ref, fit_ref, near_ref, split, places, sem, *scratch,
):
    slots, patches, unknowns = far_ref.shape
    copy = pltpu.make_async_copy(far_ref, near_ref, sem)
    copy.start()
    choose(sides, subregion, tile, cells_ref, valid_ref, nodes_ref, hot_ref, places)
    design_kernel(slots, unknowns, radius_ref, xyz_ref, design_ref, *scratch)
    copy.wait()
    spread(near_ref, split)
    for p in range(patches):
        turn(p, split, fit_ref, slots)


def design_kernel(nodes, unknowns, radius_ref, xyz_ref, design_ref, pos, ax, by, ax2, bc, bm, bl, far):
    patches = design_ref.shape[0]
    lanes = design_ref.shape[2]
    tile = (2 * LAYERS, lanes)
    pos[:, :, 0:nodes] = xyz_ref[...]
    lane = lax.broadcasted_iota(jnp.int32, (1, lanes), 1)
    is_node = lane < nodes
    used = lane < unknowns
    power = []
    for axis in range(3):
        rows = []
        for degree in range(1, 4):
            hit = lane < 0
            for index, triple in enumerate(EXPONENTS):
                if triple[axis] == degree:
                    hit = hit | (lane == nodes + index)
            rows.append(hit)
        power.append(rows)

    def raised(value, axis):
        one, two, three = power[axis]
        square = value * value
        out = jnp.where(one, value, jnp.where(used, 1.0, 0.0))
        out = jnp.where(two, square, out)
        return jnp.where(three, square * value, out)

    across = (lax.broadcasted_iota(jnp.int32, (16, lanes), 0) - REACH).astype(jnp.float32)
    layer = lax.broadcasted_iota(jnp.int32, tile, 0)
    upper = layer < LAYERS
    deep = jnp.where(upper, layer, layer - LAYERS).astype(jnp.float32) - 0.5 * (LAYERS - 1)
    tail = slice(lanes - 128, lanes)
    half = SPAN // 2

    for index, flat in enumerate(DISTANCES):
        far[index] = jnp.sqrt(float(flat) + deep[:, :128] * deep[:, :128])

    def patch(p, q):
        inverse = 1.0 / jnp.full((1, lanes), radius_ref[0, p], jnp.float32)
        x = jnp.where(is_node, pos[0, pl.ds(p, 1), :], 0.0)
        y = jnp.where(is_node, pos[1, pl.ds(p, 1), :], 0.0)
        z = jnp.where(is_node, pos[2, pl.ds(p, 1), :], 0.0)
        dx = (across - x) * inverse
        dy = (across - y) * inverse
        dz = (deep - z) * inverse
        ax[q] = jnp.where(is_node, dx * dx, raised(dx, 0))
        by[q] = jnp.where(is_node, dy * dy, raised(dy, 1))
        cz = jnp.where(is_node, dz * dz + 1e-30, raised(dz, 2))
        for i in range(half + 1):
            low, high = 2 * i, min(2 * i + 1, SPAN - 1)
            row = jnp.where(upper, by[q, low : low + 1, :], by[q, high : high + 1, :])
            bc[q, i] = row + cz
            bm[q, i] = row[:, tail] * cz[:, tail]
            ax2[q, i] = jnp.where(upper, ax[q, low : low + 1, :], ax[q, high : high + 1, :])
        for index, flat in enumerate(DISTANCES):
            rho = far[index] * inverse[:, :128]
            left = jnp.maximum(1.0 - rho, 0.0)
            left = left * left
            bl[q, index] = left * left * (4.0 * rho + 1.0)

        def pair(spots):
            (ex, ey), (fx, fy) = spots[0], spots[-1]
            row = ax[q, ex : ex + 1, :] if ex == fx else ax2[q, ex // 2]
            part = row + bc[q, ey // 2]
            part = part * part * lax.rsqrt(part)
            last = row[:, tail] * bm[q, ey // 2]
            blend = [bl[q, DISTANCES.index((i - REACH) ** 2 + (j - REACH) ** 2)] for i, j in ((ex, ey), (fx, fy))]
            blend = blend[0] if (ex, ey) == (fx, fy) else jnp.where(upper[:, :128], blend[0], blend[1])
            if len(spots) == 1:
                blend = jnp.where(upper[:, :128], blend, 0.0)
            pieces = [part[:, c : c + 128] for c in range(0, lanes, 128)]
            pieces[-1] = jnp.where(is_node[:, tail], pieces[-1], last)
            return jnp.concatenate([piece * blend for piece in pieces], 1)

        for spot in range(0, len(SPOTS), 4):
            rows = [pair(SPOTS[r : r + 2]) if r < len(SPOTS) else jnp.zeros(tile, jnp.float32) for r in (spot, spot + 2)]
            design_ref[p, spot * LAYERS : (spot + 4) * LAYERS, :] = jnp.concatenate(rows, 0).astype(jnp.bfloat16)

    for p in range(patches):
        patch(p, p % LOOKS)


def spread(fit_ref, wide):
    slots, patches, unknowns = fit_ref.shape
    for c in range(0, unknowns, 128):
        width = min(128, unknowns - c)
        wide[c // 128, :, :width] = fit_ref[:, :, c : c + width].astype(jnp.float32).reshape(slots * patches, width)


def turn(p, wide, fit, slots):
    patches, unknowns, padded = fit.shape
    for c in range(0, unknowns, 128):
        width = min(128, unknowns - c)
        piece = wide[c // 128, pl.ds(p, slots, stride=patches), :].astype(fit.dtype)
        fit[p, c : c + width, 0:slots] = piece.T[:width]
        fit[p, c : c + width, slots:padded] = jnp.zeros((width, padded - slots), fit.dtype)


def choose(sides, subregion, tile, cells_ref, valid_ref, nodes_ref, hot, places):
    patches, slots = nodes_ref.shape
    padded = hot.shape[1]
    kind = hot.dtype
    lane = lax.broadcasted_iota(jnp.int32, (1, slots), 1)
    places[...] = jnp.full(places.shape, -1.0, jnp.float32)
    for p in range(patches):
        index = nodes_ref[p : p + 1, :]
        where = lax.div(index, jnp.int32(subregion))
        a = jnp.zeros_like(where)
        for t in range(1, sides[0] + 2):
            a = a + jnp.where(where >= t * (sides[1] + 2), 1, 0)
        b = where - a * (sides[1] + 2)
        home_x, home_y = home(sides, tile, cells_ref, p)
        local = (a - home_x) * NEAR + (b - home_y)
        local = jnp.where(lane < valid_ref[0, p], local, -1)
        places[0, p : p + 1, 0:slots] = (index - where * subregion).astype(jnp.float32)
        places[1, p : p + 1, 0:slots] = local.astype(jnp.float32)
    inner, local = places[0].T, places[1].T
    node = lax.broadcasted_iota(jnp.int32, (padded, subregion), 1).astype(jnp.float32).astype(kind)
    one, zero = jnp.ones((), kind), jnp.zeros((), kind)
    for p in range(patches):
        column = jnp.broadcast_to(inner[:padded, p : p + 1], (padded, subregion)).astype(kind)
        one_hot = jnp.where(node == column, one, zero)
        column = jnp.broadcast_to(local[:padded, p : p + 1], (padded, subregion)).astype(kind)
        for s in range(NEAR * NEAR):
            hot[p, :, s * subregion : (s + 1) * subregion] = jnp.where(column == jnp.full((), s, kind), one_hot, zero)


def home(sides, tile, cells_ref, p):
    return (cells_ref[0, 0, p] * sides[0]) // tile[0], (cells_ref[1, 0, p] * sides[1]) // tile[1]


def sample_kernel(
    tile, cells_ref, own_ref, b_ref, c_ref, d_ref, hot_ref, out_ref, near,
):
    sx, sy, subregion, fields = own_ref.shape
    odd_x, odd_y = parity()
    xa = (1 - odd_x) * (sx + 1)
    xb = odd_x * (sx + 1)
    ya = (1 - odd_y) * (sy + 1)
    yb = odd_y * (sy + 1)
    near[1 : sx + 1, 1 : sy + 1] = own_ref[...]
    near[xb, 1 : sy + 1] = b_ref[...]
    near[1 : sx + 1, ya] = c_ref[...]
    near[1 : sx + 1, yb] = d_ref[...]
    near[xb, ya] = jnp.zeros(near.shape[2:], near.dtype)
    near[xb, yb] = jnp.zeros(near.shape[2:], near.dtype)
    near[xa] = jnp.zeros(near.shape[1:], near.dtype)
    for p in range(hot_ref.shape[0]):
        home_x, home_y = home((sx, sy), tile, cells_ref, p)
        window = jnp.concatenate(
            [near[home_x + r, pl.ds(home_y, NEAR)].reshape(NEAR * subregion, fields) for r in range(NEAR)], 0
        )
        out_ref[p] = jnp.dot(hot_ref[p], window, preferred_element_type=jnp.float32).astype(out_ref.dtype)


def blend_kernel(
    sides, tile, cells_ref, side_ref, ea_ref, eb_ref, sample_ref, hot_ref, fit_ref, design_ref,
    inner_ref, xa_ref, xb_ref, da_ref, db_ref, za_ref, zb_ref, edges, chosen, coeffs, values, acc,
):
    sx, sy = sides
    subregion, fields = side_ref.shape[1:]
    patches, unknowns, _ = fit_ref.shape
    cx, cy = tile
    rows = len(SPOTS) * LAYERS
    odd_x, odd_y = parity()
    xa, xb = (1 - odd_x) * (sx + 1), odd_x * (sx + 1)
    acc[...] = jnp.zeros_like(acc)
    edges[0] = side_ref[...]
    edges[1, 1 : sy + 1] = jnp.zeros((sy, subregion, fields), edges.dtype)
    edges[1, (1 - odd_y) * (sy + 1)] = ea_ref[...]
    edges[1, odd_y * (sy + 1)] = eb_ref[...]
    for p in range(patches):
        home_x, home_y = home(sides, tile, cells_ref, p)
        turn = jnp.where(jnp.abs(xa - home_x - 1) <= 1, 0, 1)
        row = jnp.where(turn == 0, xa, xb) - home_x
        here = (row >= 0) & (row < NEAR)
        spot = pl.multiple_of(jnp.where(here, row, 0) * (NEAR * subregion), NEAR * subregion)
        edge = edges[turn, pl.ds(home_y, NEAR)].reshape(NEAR * subregion, fields)
        edge = edge * jnp.where(here, 1.0, 0.0).astype(edge.dtype)
        extra = jnp.dot(hot_ref[p, :, pl.ds(spot, NEAR * subregion)], edge, preferred_element_type=jnp.float32)
        chosen[p] = sample_ref[p] + extra.astype(chosen.dtype)
    for p in range(patches):
        coeffs[p] = jnp.dot(fit_ref[p], chosen[p], preferred_element_type=jnp.float32).astype(coeffs.dtype)

    def place(p):
        first, second, third = cells_ref[0, 0, p], cells_ref[1, 0, p], cells_ref[2, 0, p]
        for s, (ex, ey) in enumerate(SPOTS):
            for l in range(acc.shape[0]):
                spot = (l, first + ex, second + ey, pl.ds(third, LAYERS))
                acc[spot] = acc[spot] + values[p, s * LAYERS : (s + 1) * LAYERS, l * 128 : (l + 1) * 128]

    for p in range(patches):
        values[p] = jnp.dot(design_ref[p, :rows, :unknowns], coeffs[p], preferred_element_type=jnp.float32)
        if p:
            place(p - 1)
    place(patches - 1)

    ra = (1 - odd_x) * (cx + REACH)
    rb = odd_x * (cx + REACH)
    sa = (1 - odd_y) * (cy + REACH)
    sb = odd_y * (cy + REACH)
    rim, in_x, in_y = REACH, pl.ds(REACH, cx), pl.ds(REACH, cy)
    for l in range(acc.shape[0]):
        f = pl.ds(l * 128, 128)
        xa_ref[:, :, :, f] = acc[l, pl.ds(ra, rim)].astype(xa_ref.dtype)
        xb_ref[:, :, :, f] = acc[l, pl.ds(rb, rim), in_y].astype(xb_ref.dtype)
        for ref, s, turn in ((da_ref, sa, 0), (db_ref, sb, 1)):
            ref[:, :, :, f] = (acc[l, pl.ds(rb, rim), pl.ds(s, rim)] * paired(turn)).astype(ref.dtype)
        for ref, s in ((za_ref, sa), (zb_ref, sb)):
            ref[:, :, :, f] = acc[l, in_x, pl.ds(s, rim)]
        inner_ref[:, :, :, f] = acc[l, in_x, in_y]


def relay_kernel(za_ref, zb_ref, xa_ref, outa_ref, outb_ref):
    odd_x, odd_y = parity()
    cx = za_ref.shape[0]
    rows = pl.ds((1 - odd_x) * (cx - REACH), REACH)
    last = xa_ref.shape[1] - REACH
    for z_ref, out_ref, s, turn in ((za_ref, outa_ref, (1 - odd_y) * last, 0), (zb_ref, outb_ref, odd_y * last, 1)):
        keep = paired(turn)
        out_ref[...] = (z_ref[...] * keep).astype(out_ref.dtype)
        got = xa_ref[:, pl.ds(s, REACH)].astype(jnp.float32)
        out_ref[rows] = ((z_ref[rows] + got) * keep).astype(out_ref.dtype)


def gather_kernel(inner_ref, scale_ref, xa_ref, xb_ref, za_ref, zb_ref, out_ref, wide_ref):
    cx, cy, depth, fields = inner_ref.shape
    for i in range(cx):
        columns = scale_ref[i]
        for j in range(cy):
            wide_ref[i, j] = jnp.broadcast_to(columns[:, j : j + 1], wide_ref.shape[2:])
    odd_x, odd_y = parity()
    far, back = pl.ds((1 - odd_x) * (cx - REACH), REACH), pl.ds(odd_x * (cx - REACH), REACH)
    for f in range(0, fields, 128):
        part = slice(f, f + 128)
        out_ref[:, :, :, part] = inner_ref[:, :, :, part] * wide_ref[...]
        got = xa_ref[:, REACH : REACH + cy, :, part].astype(jnp.float32)
        out_ref[far, :, :, part] = out_ref[far, :, :, part] + got * wide_ref[far]
        got = xb_ref[:, :, :, part].astype(jnp.float32)
        out_ref[back, :, :, part] = out_ref[back, :, :, part] + got * wide_ref[back]
        for z_ref, s in ((za_ref, (1 - odd_y) * (cy - REACH)), (zb_ref, odd_y * (cy - REACH))):
            spot = (slice(None), pl.ds(s, REACH))
            got = z_ref[:, :, :, part].astype(jnp.float32)
            out_ref[spot + (slice(None), part)] = out_ref[spot + (slice(None), part)] + got * wide_ref[spot]


def finish_kernel(base_ref, wide_ref, da_ref, db_ref, out_ref):
    cx, cy, depth, fields = base_ref.shape
    odd_x, odd_y = parity()
    back = pl.ds(odd_x * (cx - REACH), REACH)
    for f in range(0, fields, 128):
        part = slice(f, f + 128)
        out_ref[:, :, :, part] = base_ref[:, :, :, part].astype(out_ref.dtype)
        for d_ref, s in ((da_ref, (1 - odd_y) * (cy - REACH)), (db_ref, odd_y * (cy - REACH))):
            spot = (back, pl.ds(s, REACH))
            got = d_ref[:, :, :, part].astype(jnp.float32) * wide_ref[spot]
            out_ref[spot + (slice(None), part)] = (base_ref[spot + (slice(None), part)] + got).astype(out_ref.dtype)


def params(megabytes):
    return pltpu.CompilerParams(vmem_limit_bytes=megabytes * 2**20)


def local(node_values, fit_ops, node_xyz, patch_nodes, patch_valid, patch_cell, patch_radius, cell_scale):
    sx, sy, subregion, fields = node_values.shape
    patches, unknowns, slots = fit_ops.shape[2:]
    cx, cy, depth = cell_scale.shape
    across, along = lax.axis_size("gx"), lax.axis_size("gy")
    kind = node_values.dtype
    full = jnp.float32
    shape = jax.ShapeDtypeStruct
    lanes = up(unknowns, 128)
    rows = up(len(SPOTS), 4) * LAYERS
    halves = fields // 128

    def send(block, turn_x, turn_y):
        return lax.ppermute(block, ("gx", "gy"), routes(across, along, turn_x, turn_y))

    def send_x(block, turn):
        return send(block, turn, None)

    def send_y(block, turn):
        return send(block, None, turn)

    def send_across(block, turn):
        return send(block, 1, turn)

    line = lambda *sides: shape(sides + (subregion, fields), kind)
    plain = (
        patch_cell.transpose(0, 3, 1, 2)[0],
        patch_valid[0],
        patch_nodes[0, 0],
        patch_radius[0],
        node_xyz[0, 0].transpose(1, 0, 2),
        cell_scale.transpose(0, 2, 1),
    )
    packed = pl.pallas_call(
        lambda *refs: pack_kernel(len(plain), *refs),
        out_shape=(line(sx), line(sx), line(sy), line(sy), line(), line()) + tuple(shape(x.shape, x.dtype) for x in plain),
        in_specs=[pl.BlockSpec(memory_space=pl.ANY)] * (1 + len(plain)),
        out_specs=(VMEM,) * (6 + len(plain)),
        scratch_shapes=[pltpu.SemaphoreType.DMA((6 + len(plain),))],
        compiler_params=params(4),
        cost_estimate=SMALL,
        name="pack",
    )(*[pltpu.with_memory_space_constraint(x, pltpu.HBM) for x in (node_values, *plain)])
    to_ya, to_yb, to_xa, to_xb, to_da, to_db, cells, valid, indices, radius, xyz, scale = packed
    from_ya = send_y(to_ya, 0)
    from_yb = send_y(to_yb, 1)
    from_xb = send_x(to_xb, 1)
    from_da = send_across(to_da, 0)
    from_db = send_across(to_db, 1)
    window = NEAR * NEAR * subregion
    padded = up(slots, 16)
    far = pltpu.with_memory_space_constraint(fit_ops[0, 0].transpose(2, 0, 1), pltpu.HBM)
    design, hot, fit = pl.pallas_call(
        lambda *refs: prepare_kernel((sx, sy), subregion, (cx, cy), *refs),
        out_shape=(
            shape((patches, rows, lanes), kind),
            shape((patches, padded, window), kind),
            shape((patches, unknowns, padded), kind),
        ),
        in_specs=[SMEM, VMEM, SMEM, SMEM, VMEM, pl.BlockSpec(memory_space=pl.ANY)],
        out_specs=(VMEM,) * 3,
        scratch_shapes=[
            pltpu.VMEM(far.shape, kind),
            pltpu.VMEM((lanes // 128, slots * patches, 128), full),
            pltpu.VMEM((2, patches, up(padded, 128)), full),
            pltpu.SemaphoreType.DMA,
            pltpu.VMEM((3, patches, lanes), full),
            pltpu.VMEM((LOOKS, 16, lanes), full),
            pltpu.VMEM((LOOKS, 16, lanes), full),
            pltpu.VMEM((LOOKS, SPAN // 2 + 1, 2 * LAYERS, lanes), full),
            pltpu.VMEM((LOOKS, SPAN // 2 + 1, 2 * LAYERS, lanes), full),
            pltpu.VMEM((LOOKS, SPAN // 2 + 1, 2 * LAYERS, 128), full),
            pltpu.VMEM((LOOKS, len(DISTANCES), 2 * LAYERS, 128), full),
            pltpu.VMEM((len(DISTANCES), 2 * LAYERS, 128), full),
        ],
        compiler_params=params(24),
        cost_estimate=SMALL,
        name="prepare",
    )(radius, xyz, cells, valid, indices, far)
    from_xb, from_yb, from_ya, hot = lax.optimization_barrier((from_xb, from_yb, from_ya, hot))
    to_xa = pl.pallas_call(
        extend_kernel,
        out_shape=line(sy + 2),
        in_specs=[VMEM] * 3,
        out_specs=VMEM,
        compiler_params=params(4),
        cost_estimate=SMALL,
        name="extend",
    )(from_ya, from_yb, to_xa)
    from_xa = send_x(to_xa, 0)
    samples = pl.pallas_call(
        lambda *refs: sample_kernel((cx, cy), *refs),
        out_shape=shape((patches, padded, fields), kind),
        in_specs=[SMEM] + [VMEM] * 5,
        out_specs=VMEM,
        scratch_shapes=[pltpu.VMEM((sx + 2, sy + 2, subregion, fields), kind)],
        compiler_params=params(16),
        cost_estimate=LARGE,
        name="sample",
    )(cells, node_values, from_xb, from_ya, from_yb, hot)

    block = lambda *dims, kind=kind: shape(dims + (depth, fields), kind)
    inner, xa, xb, da, db, za, zb = pl.pallas_call(
        lambda *refs: blend_kernel((sx, sy), (cx, cy), *refs),
        out_shape=(
            block(cx, cy, kind=full),
            block(REACH, cy + 2 * REACH),
            block(REACH, cy),
            block(REACH, REACH),
            block(REACH, REACH),
            block(cx, REACH, kind=full),
            block(cx, REACH, kind=full),
        ),
        in_specs=[SMEM] + [VMEM] * 7,
        out_specs=(VMEM,) * 7,
        scratch_shapes=[
            pltpu.VMEM((2, sy + 2, subregion, fields), kind),
            pltpu.VMEM((patches, padded, fields), kind),
            pltpu.VMEM((patches, unknowns, fields), kind),
            pltpu.VMEM((patches, len(SPOTS) * LAYERS, fields), full),
            pltpu.VMEM((halves, cx + 2 * REACH, cy + 2 * REACH, depth, 128), full),
        ],
        compiler_params=params(32),
        cost_estimate=SMALL,
        name="blend",
    )(cells, from_xa, from_da, from_db, samples, hot, fit, design)

    got_xa = send_x(xa, 0)
    got_xb = send_x(xb, 1)
    got_db = send_across(db, 1)
    got_da = send_across(da, 0)
    za, zb = pl.pallas_call(
        relay_kernel,
        out_shape=(block(cx, REACH), block(cx, REACH)),
        in_specs=[VMEM] * 3,
        out_specs=(VMEM, VMEM),
        compiler_params=params(8),
        cost_estimate=SMALL,
        name="relay",
    )(za, zb, got_xa)
    got_za = send_y(za, 0)
    got_zb = send_y(zb, 1)
    base, wide = pl.pallas_call(
        gather_kernel,
        out_shape=(block(cx, cy, kind=full), shape((cx, cy, depth, 128), full)),
        in_specs=[VMEM] * 6,
        out_specs=(VMEM, VMEM),
        compiler_params=params(12),
        cost_estimate=LARGE,
        name="gather",
    )(inner, scale, got_xa, got_xb, got_za, got_zb)
    return pl.pallas_call(
        finish_kernel,
        out_shape=block(cx, cy),
        in_specs=[VMEM] * 4,
        out_specs=VMEM,
        compiler_params=params(12),
        cost_estimate=SMALL,
        name="finish",
    )(base, wide, got_da, got_db)


def solution(mesh):
    placed = (
        P("gx", "gy", None, None),
        P("gx", "gy", None, None, None),
        P("gx", "gy", None, None, None),
        P("gx", "gy", None, None),
        P("gx", "gy", None),
        P("gx", "gy", None, None),
        P("gx", "gy", None),
        P("gx", "gy", None),
    )
    return jax.shard_map(
        local, mesh=mesh, in_specs=placed, out_specs=P("gx", "gy", None, None), check_vma=False
    )
```

```python
import jax
import jax.numpy as jnp
from jax import lax
from jax.experimental import pallas as pl
from jax.experimental.pallas import tpu as pltpu
from jax.sharding import PartitionSpec as P

REACH = 4
SPAN = 2 * REACH + 1
LAYERS = 4
NEAR = 3
LOOKS = 2
EXPONENTS = (
    (0, 0, 0),
    (1, 0, 0),
    (0, 1, 0),
    (0, 0, 1),
    (2, 0, 0),
    (1, 1, 0),
    (1, 0, 1),
    (0, 2, 0),
    (0, 1, 1),
    (0, 0, 2),
    (3, 0, 0),
    (2, 1, 0),
    (2, 0, 1),
    (1, 2, 0),
    (1, 1, 1),
    (1, 0, 2),
    (0, 3, 0),
    (0, 2, 1),
    (0, 1, 2),
    (0, 0, 3),
)
DISTANCES = sorted({a * a + b * b for a in range(REACH + 1) for b in range(REACH + 1)})
SPOTS = [(ex, ey) for ex in range(SPAN) for ey in range(SPAN - 1)] + [(ex, SPAN - 1) for ex in range(SPAN)]
VMEM = pl.BlockSpec(memory_space=pltpu.VMEM)
SMEM = pl.BlockSpec(memory_space=pltpu.SMEM)


SMALL = pl.CostEstimate(flops=1000, bytes_accessed=1000, transcendentals=0)
LARGE = pl.CostEstimate(flops=4_000_000_000, bytes_accessed=40_000_000, transcendentals=0)


def up(value, multiple):
    return -(-value // multiple) * multiple


def parity():
    return lax.rem(lax.axis_index("gx"), 2), lax.rem(lax.axis_index("gy"), 2)


def partner(i, size, turn, wrap):
    j = i + 1 if i % 2 == turn else i - 1
    return j % size if wrap or 0 <= j < size else None


def routes(across, along, turn_x, turn_y):
    pairs = []
    for i in range(across):
        for j in range(along):
            to = i if turn_x is None else partner(i, across, turn_x, True)
            up_to = j if turn_y is None else partner(j, along, turn_y, False)
            if up_to is None:
                to, up_to = partner(i, across, 0, True), j
            pairs.append((i * along + j, to * along + up_to))
    return pairs


def paired(turn):
    j, odd = lax.axis_index("gy"), parity()[1]
    to = jnp.where(odd == turn, j + 1, j - 1)
    return jnp.where((to >= 0) & (to < lax.axis_size("gy")), 1.0, 0.0).astype(jnp.float32)


def pack_kernel(count, nodes_ref, *refs):
    plain, sent, copied, sems = refs[:count], refs[count : count + 6], refs[count + 6 : -1], refs[-1]
    ya_ref, yb_ref, xa_ref, xb_ref, da_ref, db_ref = sent
    sx, sy = nodes_ref.shape[:2]
    odd_x, odd_y = parity()
    far_x, back_x = (1 - odd_x) * (sx - 1), odd_x * (sx - 1)
    far_y, back_y = (1 - odd_y) * (sy - 1), odd_y * (sy - 1)
    pairs = (
        (nodes_ref.at[back_x, back_y], db_ref),
        (nodes_ref.at[back_x, far_y], da_ref),
        (nodes_ref.at[:, far_y], ya_ref),
        (nodes_ref.at[:, back_y], yb_ref),
        (nodes_ref.at[back_x], xb_ref),
        (nodes_ref.at[far_x], xa_ref),
        *zip(plain, copied),
    )
    copies = [pltpu.make_async_copy(source, target, sems.at[index]) for index, (source, target) in enumerate(pairs)]
    for copy in copies:
        copy.start()
    for copy in copies:
        copy.wait()


def extend_kernel(ya_ref, yb_ref, own_ref, out_ref):
    odd_x, odd_y = parity()
    far_x = (1 - odd_x) * (ya_ref.shape[0] - 1)
    last = out_ref.shape[0] - 1
    out_ref[1:last] = own_ref[...]
    out_ref[(1 - odd_y) * last] = ya_ref[far_x]
    out_ref[odd_y * last] = yb_ref[far_x]


def prepare_kernel(
    sides, subregion, tile, radius_ref, xyz_ref, cells_ref, valid_ref, nodes_ref, far_ref,
    design_ref, hot_ref, fit_ref, near_ref, split, places, sem, *scratch,
):
    slots, patches, unknowns = far_ref.shape
    copy = pltpu.make_async_copy(far_ref, near_ref, sem)
    copy.start()
    choose(sides, subregion, tile, cells_ref, valid_ref, nodes_ref, hot_ref, places)
    design_kernel(slots, unknowns, radius_ref, xyz_ref, design_ref, *scratch)
    copy.wait()
    spread(near_ref, split)
    for p in range(patches):
        turn(p, split, fit_ref, slots)


def design_kernel(nodes, unknowns, radius_ref, xyz_ref, design_ref, pos, ax, by, ax2, bc, bm, bl, far):
    patches = design_ref.shape[0]
    lanes = design_ref.shape[2]
    tile = (2 * LAYERS, lanes)
    pos[:, :, 0:nodes] = xyz_ref[...]
    lane = lax.broadcasted_iota(jnp.int32, (1, lanes), 1)
    is_node = lane < nodes
    used = lane < unknowns
    power = []
    for axis in range(3):
        rows = []
        for degree in range(1, 4):
            hit = lane < 0
            for index, triple in enumerate(EXPONENTS):
                if triple[axis] == degree:
                    hit = hit | (lane == nodes + index)
            rows.append(hit)
        power.append(rows)

    def raised(value, axis):
        one, two, three = power[axis]
        square = value * value
        out = jnp.where(one, value, jnp.where(used, 1.0, 0.0))
        out = jnp.where(two, square, out)
        return jnp.where(three, square * value, out)

    across = (lax.broadcasted_iota(jnp.int32, (16, lanes), 0) - REACH).astype(jnp.float32)
    layer = lax.broadcasted_iota(jnp.int32, tile, 0)
    upper = layer < LAYERS
    deep = jnp.where(upper, layer, layer - LAYERS).astype(jnp.float32) - 0.5 * (LAYERS - 1)
    tail = slice(lanes - 128, lanes)
    half = SPAN // 2

    for index, flat in enumerate(DISTANCES):
        far[index] = jnp.sqrt(float(flat) + deep[:, :128] * deep[:, :128])

    def patch(p, q):
        inverse = 1.0 / jnp.full((1, lanes), radius_ref[0, p], jnp.float32)
        x = jnp.where(is_node, pos[0, pl.ds(p, 1), :], 0.0)
        y = jnp.where(is_node, pos[1, pl.ds(p, 1), :], 0.0)
        z = jnp.where(is_node, pos[2, pl.ds(p, 1), :], 0.0)
        dx = (across - x) * inverse
        dy = (across - y) * inverse
        dz = (deep - z) * inverse
        ax[q] = jnp.where(is_node, dx * dx, raised(dx, 0))
        by[q] = jnp.where(is_node, dy * dy, raised(dy, 1))
        cz = jnp.where(is_node, dz * dz + 1e-30, raised(dz, 2))
        for i in range(half + 1):
            low, high = 2 * i, min(2 * i + 1, SPAN - 1)
            row = jnp.where(upper, by[q, low : low + 1, :], by[q, high : high + 1, :])
            bc[q, i] = row + cz
            bm[q, i] = row[:, tail] * cz[:, tail]
            ax2[q, i] = jnp.where(upper, ax[q, low : low + 1, :], ax[q, high : high + 1, :])
        for index, flat in enumerate(DISTANCES):
            rho = far[index] * inverse[:, :128]
            left = jnp.maximum(1.0 - rho, 0.0)
            left = left * left
            bl[q, index] = left * left * (4.0 * rho + 1.0)

        def pair(spots):
            (ex, ey), (fx, fy) = spots[0], spots[-1]
            row = ax[q, ex : ex + 1, :] if ex == fx else ax2[q, ex // 2]
            part = row + bc[q, ey // 2]
            part = part * part * lax.rsqrt(part)
            last = row[:, tail] * bm[q, ey // 2]
            blend = [bl[q, DISTANCES.index((i - REACH) ** 2 + (j - REACH) ** 2)] for i, j in ((ex, ey), (fx, fy))]
            blend = blend[0] if (ex, ey) == (fx, fy) else jnp.where(upper[:, :128], blend[0], blend[1])
            if len(spots) == 1:
                blend = jnp.where(upper[:, :128], blend, 0.0)
            pieces = [part[:, c : c + 128] for c in range(0, lanes, 128)]
            pieces[-1] = jnp.where(is_node[:, tail], pieces[-1], last)
            return jnp.concatenate([piece * blend for piece in pieces], 1)

        for spot in range(0, len(SPOTS), 4):
            rows = [pair(SPOTS[r : r + 2]) if r < len(SPOTS) else jnp.zeros(tile, jnp.float32) for r in (spot, spot + 2)]
            design_ref[p, spot * LAYERS : (spot + 4) * LAYERS, :] = jnp.concatenate(rows, 0).astype(jnp.bfloat16)

    for p in range(patches):
        patch(p, p % LOOKS)


def spread(fit_ref, wide):
    slots, patches, unknowns = fit_ref.shape
    for c in range(0, unknowns, 128):
        width = min(128, unknowns - c)
        wide[c // 128, :, :width] = fit_ref[:, :, c : c + width].astype(jnp.float32).reshape(slots * patches, width)


def turn(p, wide, fit, slots):
    patches, unknowns, padded = fit.shape
    for c in range(0, unknowns, 128):
        width = min(128, unknowns - c)
        piece = wide[c // 128, pl.ds(p, slots, stride=patches), :].astype(fit.dtype)
        fit[p, c : c + width, 0:slots] = piece.T[:width]
        fit[p, c : c + width, slots:padded] = jnp.zeros((width, padded - slots), fit.dtype)


def choose(sides, subregion, tile, cells_ref, valid_ref, nodes_ref, hot, places):
    patches, slots = nodes_ref.shape
    padded = hot.shape[1]
    kind = hot.dtype
    lane = lax.broadcasted_iota(jnp.int32, (1, slots), 1)
    places[...] = jnp.full(places.shape, -1.0, jnp.float32)
    for p in range(patches):
        index = nodes_ref[p : p + 1, :]
        where = lax.div(index, jnp.int32(subregion))
        a = jnp.zeros_like(where)
        for t in range(1, sides[0] + 2):
            a = a + jnp.where(where >= t * (sides[1] + 2), 1, 0)
        b = where - a * (sides[1] + 2)
        home_x, home_y = home(sides, tile, cells_ref, p)
        local = (a - home_x) * NEAR + (b - home_y)
        local = jnp.where(lane < valid_ref[0, p], local, -1)
        places[0, p : p + 1, 0:slots] = (index - where * subregion).astype(jnp.float32)
        places[1, p : p + 1, 0:slots] = local.astype(jnp.float32)
    inner, local = places[0].T, places[1].T
    node = lax.broadcasted_iota(jnp.int32, (padded, subregion), 1).astype(jnp.float32).astype(kind)
    one, zero = jnp.ones((), kind), jnp.zeros((), kind)
    for p in range(patches):
        column = jnp.broadcast_to(inner[:padded, p : p + 1], (padded, subregion)).astype(kind)
        one_hot = jnp.where(node == column, one, zero)
        column = jnp.broadcast_to(local[:padded, p : p + 1], (padded, subregion)).astype(kind)
        for s in range(NEAR * NEAR):
            hot[p, :, s * subregion : (s + 1) * subregion] = jnp.where(column == jnp.full((), s, kind), one_hot, zero)


def home(sides, tile, cells_ref, p):
    return (cells_ref[0, 0, p] * sides[0]) // tile[0], (cells_ref[1, 0, p] * sides[1]) // tile[1]


def sample_kernel(
    tile, cells_ref, own_ref, b_ref, c_ref, d_ref, hot_ref, out_ref, near,
):
    sx, sy, subregion, fields = own_ref.shape
    odd_x, odd_y = parity()
    xa = (1 - odd_x) * (sx + 1)
    xb = odd_x * (sx + 1)
    ya = (1 - odd_y) * (sy + 1)
    yb = odd_y * (sy + 1)
    near[1 : sx + 1, 1 : sy + 1] = own_ref[...]
    near[xb, 1 : sy + 1] = b_ref[...]
    near[1 : sx + 1, ya] = c_ref[...]
    near[1 : sx + 1, yb] = d_ref[...]
    near[xb, ya] = jnp.zeros(near.shape[2:], near.dtype)
    near[xb, yb] = jnp.zeros(near.shape[2:], near.dtype)
    near[xa] = jnp.zeros(near.shape[1:], near.dtype)
    for p in range(hot_ref.shape[0]):
        home_x, home_y = home((sx, sy), tile, cells_ref, p)
        window = jnp.concatenate(
            [near[home_x + r, pl.ds(home_y, NEAR)].reshape(NEAR * subregion, fields) for r in range(NEAR)], 0
        )
        out_ref[p] = jnp.dot(hot_ref[p], window, preferred_element_type=jnp.float32).astype(out_ref.dtype)


def blend_kernel(
    sides, tile, cells_ref, side_ref, ea_ref, eb_ref, sample_ref, hot_ref, fit_ref, design_ref,
    acc, xa_ref, xb_ref, da_ref, db_ref, edges, chosen, coeffs, values,
):
    sx, sy = sides
    subregion, fields = side_ref.shape[1:]
    patches, unknowns, _ = fit_ref.shape
    cx, cy = tile
    rows = len(SPOTS) * LAYERS
    odd_x, odd_y = parity()
    xa, xb = (1 - odd_x) * (sx + 1), odd_x * (sx + 1)
    acc[...] = jnp.zeros_like(acc)
    edges[0] = side_ref[...]
    edges[1, 1 : sy + 1] = jnp.zeros((sy, subregion, fields), edges.dtype)
    edges[1, (1 - odd_y) * (sy + 1)] = ea_ref[...]
    edges[1, odd_y * (sy + 1)] = eb_ref[...]
    for p in range(patches):
        home_x, home_y = home(sides, tile, cells_ref, p)
        turn = jnp.where(jnp.abs(xa - home_x - 1) <= 1, 0, 1)
        row = jnp.where(turn == 0, xa, xb) - home_x
        here = (row >= 0) & (row < NEAR)
        spot = pl.multiple_of(jnp.where(here, row, 0) * (NEAR * subregion), NEAR * subregion)
        edge = edges[turn, pl.ds(home_y, NEAR)].reshape(NEAR * subregion, fields)
        edge = edge * jnp.where(here, 1.0, 0.0).astype(edge.dtype)
        extra = jnp.dot(hot_ref[p, :, pl.ds(spot, NEAR * subregion)], edge, preferred_element_type=jnp.float32)
        chosen[p] = sample_ref[p] + extra.astype(chosen.dtype)
    for p in range(patches):
        coeffs[p] = jnp.dot(fit_ref[p], chosen[p], preferred_element_type=jnp.float32).astype(coeffs.dtype)

    def place(p):
        first, second, third = cells_ref[0, 0, p], cells_ref[1, 0, p], cells_ref[2, 0, p]
        for s, (ex, ey) in enumerate(SPOTS):
            for l in range(acc.shape[0]):
                spot = (l, first + ex, second + ey, pl.ds(third, LAYERS))
                acc[spot] = acc[spot] + values[p, s * LAYERS : (s + 1) * LAYERS, l * 128 : (l + 1) * 128]

    for p in range(patches):
        values[p] = jnp.dot(design_ref[p, :rows, :unknowns], coeffs[p], preferred_element_type=jnp.float32)
        if p:
            place(p - 1)
    place(patches - 1)

    ra = (1 - odd_x) * (cx + REACH)
    rb = odd_x * (cx + REACH)
    sa = (1 - odd_y) * (cy + REACH)
    sb = odd_y * (cy + REACH)
    rim, in_y = REACH, pl.ds(REACH, cy)
    for l in range(acc.shape[0]):
        f = pl.ds(l * 128, 128)
        xa_ref[:, :, :, f] = acc[l, pl.ds(ra, rim)].astype(xa_ref.dtype)
        xb_ref[:, :, :, f] = acc[l, pl.ds(rb, rim), in_y].astype(xb_ref.dtype)
        for ref, s, turn in ((da_ref, sa, 0), (db_ref, sb, 1)):
            ref[:, :, :, f] = (acc[l, pl.ds(rb, rim), pl.ds(s, rim)] * paired(turn)).astype(ref.dtype)


def relay_kernel(acc_ref, xa_ref, outa_ref, outb_ref):
    odd_x, odd_y = parity()
    cx = outa_ref.shape[0]
    rows = pl.ds((1 - odd_x) * (cx - REACH), REACH)
    last = xa_ref.shape[1] - REACH
    for out_ref, s, turn in ((outa_ref, (1 - odd_y) * last, 0), (outb_ref, odd_y * last, 1)):
        keep = paired(turn)
        columns = pl.ds(s, REACH)
        for l in range(acc_ref.shape[0]):
            f = slice(l * 128, (l + 1) * 128)
            out_ref[:, :, :, f] = (acc_ref[l, pl.ds(REACH, cx), columns] * keep).astype(out_ref.dtype)
            mine = acc_ref[l, pl.ds((1 - odd_x) * (cx - REACH) + REACH, REACH), columns]
            got = xa_ref[:, columns, :, f].astype(jnp.float32)
            out_ref[rows, :, :, f] = ((mine + got) * keep).astype(out_ref.dtype)


def gather_kernel(acc_ref, scale_ref, xa_ref, xb_ref, za_ref, zb_ref, out_ref, wide_ref):
    cx, cy, depth, fields = out_ref.shape
    for i in range(cx):
        columns = scale_ref[i]
        for j in range(cy):
            wide_ref[i, j] = jnp.broadcast_to(columns[:, j : j + 1], wide_ref.shape[2:])
    odd_x, odd_y = parity()
    far, back = pl.ds((1 - odd_x) * (cx - REACH), REACH), pl.ds(odd_x * (cx - REACH), REACH)
    for f in range(0, fields, 128):
        part = slice(f, f + 128)
        out_ref[:, :, :, part] = acc_ref[f // 128, REACH : REACH + cx, REACH : REACH + cy] * wide_ref[...]
        got = xa_ref[:, REACH : REACH + cy, :, part].astype(jnp.float32)
        out_ref[far, :, :, part] = out_ref[far, :, :, part] + got * wide_ref[far]
        got = xb_ref[:, :, :, part].astype(jnp.float32)
        out_ref[back, :, :, part] = out_ref[back, :, :, part] + got * wide_ref[back]
        for z_ref, s in ((za_ref, (1 - odd_y) * (cy - REACH)), (zb_ref, odd_y * (cy - REACH))):
            spot = (slice(None), pl.ds(s, REACH))
            got = z_ref[:, :, :, part].astype(jnp.float32)
            out_ref[spot + (slice(None), part)] = out_ref[spot + (slice(None), part)] + got * wide_ref[spot]


def finish_kernel(base_ref, wide_ref, da_ref, db_ref, out_ref):
    cx, cy, depth, fields = base_ref.shape
    odd_x, odd_y = parity()
    back = pl.ds(odd_x * (cx - REACH), REACH)
    for f in range(0, fields, 128):
        part = slice(f, f + 128)
        out_ref[:, :, :, part] = base_ref[:, :, :, part].astype(out_ref.dtype)
        for d_ref, s in ((da_ref, (1 - odd_y) * (cy - REACH)), (db_ref, odd_y * (cy - REACH))):
            spot = (back, pl.ds(s, REACH))
            got = d_ref[:, :, :, part].astype(jnp.float32) * wide_ref[spot]
            out_ref[spot + (slice(None), part)] = (base_ref[spot + (slice(None), part)] + got).astype(out_ref.dtype)


def params(megabytes):
    return pltpu.CompilerParams(vmem_limit_bytes=megabytes * 2**20)


def local(node_values, fit_ops, node_xyz, patch_nodes, patch_valid, patch_cell, patch_radius, cell_scale):
    sx, sy, subregion, fields = node_values.shape
    patches, unknowns, slots = fit_ops.shape[2:]
    cx, cy, depth = cell_scale.shape
    across, along = lax.axis_size("gx"), lax.axis_size("gy")
    kind = node_values.dtype
    full = jnp.float32
    shape = jax.ShapeDtypeStruct
    lanes = up(unknowns, 128)
    rows = up(len(SPOTS), 4) * LAYERS
    halves = fields // 128

    def send(block, turn_x, turn_y):
        return lax.ppermute(block, ("gx", "gy"), routes(across, along, turn_x, turn_y))

    def send_x(block, turn):
        return send(block, turn, None)

    def send_y(block, turn):
        return send(block, None, turn)

    def send_across(block, turn):
        return send(block, 1, turn)

    line = lambda *sides: shape(sides + (subregion, fields), kind)
    plain = (
        patch_cell.transpose(0, 3, 1, 2)[0],
        patch_valid[0],
        patch_nodes[0, 0],
        patch_radius[0],
        node_xyz[0, 0].transpose(1, 0, 2),
        cell_scale.transpose(0, 2, 1),
    )
    packed = pl.pallas_call(
        lambda *refs: pack_kernel(len(plain), *refs),
        out_shape=(line(sx), line(sx), line(sy), line(sy), line(), line()) + tuple(shape(x.shape, x.dtype) for x in plain),
        in_specs=[pl.BlockSpec(memory_space=pl.ANY)] * (1 + len(plain)),
        out_specs=(VMEM,) * (6 + len(plain)),
        scratch_shapes=[pltpu.SemaphoreType.DMA((6 + len(plain),))],
        compiler_params=params(4),
        cost_estimate=SMALL,
        name="pack",
    )(*[pltpu.with_memory_space_constraint(x, pltpu.HBM) for x in (node_values, *plain)])
    to_ya, to_yb, to_xa, to_xb, to_da, to_db, cells, valid, indices, radius, xyz, scale = packed
    from_ya = send_y(to_ya, 0)
    from_yb = send_y(to_yb, 1)
    from_xb = send_x(to_xb, 1)
    from_da = send_across(to_da, 0)
    from_db = send_across(to_db, 1)
    window = NEAR * NEAR * subregion
    padded = up(slots, 16)
    far = pltpu.with_memory_space_constraint(fit_ops[0, 0].transpose(2, 0, 1), pltpu.HBM)
    design, hot, fit = pl.pallas_call(
        lambda *refs: prepare_kernel((sx, sy), subregion, (cx, cy), *refs),
        out_shape=(
            shape((patches, rows, lanes), kind),
            shape((patches, padded, window), kind),
            shape((patches, unknowns, padded), kind),
        ),
        in_specs=[SMEM, VMEM, SMEM, SMEM, VMEM, pl.BlockSpec(memory_space=pl.ANY)],
        out_specs=(VMEM,) * 3,
        scratch_shapes=[
            pltpu.VMEM(far.shape, kind),
            pltpu.VMEM((lanes // 128, slots * patches, 128), full),
            pltpu.VMEM((2, patches, up(padded, 128)), full),
            pltpu.SemaphoreType.DMA,
            pltpu.VMEM((3, patches, lanes), full),
            pltpu.VMEM((LOOKS, 16, lanes), full),
            pltpu.VMEM((LOOKS, 16, lanes), full),
            pltpu.VMEM((LOOKS, SPAN // 2 + 1, 2 * LAYERS, lanes), full),
            pltpu.VMEM((LOOKS, SPAN // 2 + 1, 2 * LAYERS, lanes), full),
            pltpu.VMEM((LOOKS, SPAN // 2 + 1, 2 * LAYERS, 128), full),
            pltpu.VMEM((LOOKS, len(DISTANCES), 2 * LAYERS, 128), full),
            pltpu.VMEM((len(DISTANCES), 2 * LAYERS, 128), full),
        ],
        compiler_params=params(24),
        cost_estimate=SMALL,
        name="prepare",
    )(radius, xyz, cells, valid, indices, far)
    from_xb, from_yb, from_ya, hot = lax.optimization_barrier((from_xb, from_yb, from_ya, hot))
    to_xa = pl.pallas_call(
        extend_kernel,
        out_shape=line(sy + 2),
        in_specs=[VMEM] * 3,
        out_specs=VMEM,
        compiler_params=params(4),
        cost_estimate=SMALL,
        name="extend",
    )(from_ya, from_yb, to_xa)
    from_xa = send_x(to_xa, 0)
    samples = pl.pallas_call(
        lambda *refs: sample_kernel((cx, cy), *refs),
        out_shape=shape((patches, padded, fields), kind),
        in_specs=[SMEM] + [VMEM] * 5,
        out_specs=VMEM,
        scratch_shapes=[pltpu.VMEM((sx + 2, sy + 2, subregion, fields), kind)],
        compiler_params=params(16),
        cost_estimate=LARGE,
        name="sample",
    )(cells, node_values, from_xb, from_ya, from_yb, hot)

    block = lambda *dims, kind=kind: shape(dims + (depth, fields), kind)
    total, xa, xb, da, db = pl.pallas_call(
        lambda *refs: blend_kernel((sx, sy), (cx, cy), *refs),
        out_shape=(
            shape((halves, cx + 2 * REACH, cy + 2 * REACH, depth, 128), full),
            block(REACH, cy + 2 * REACH),
            block(REACH, cy),
            block(REACH, REACH),
            block(REACH, REACH),
        ),
        in_specs=[SMEM] + [VMEM] * 7,
        out_specs=(VMEM,) * 5,
        scratch_shapes=[
            pltpu.VMEM((2, sy + 2, subregion, fields), kind),
            pltpu.VMEM((patches, padded, fields), kind),
            pltpu.VMEM((patches, unknowns, fields), kind),
            pltpu.VMEM((patches, len(SPOTS) * LAYERS, fields), full),
        ],
        compiler_params=params(32),
        cost_estimate=SMALL,
        name="blend",
    )(cells, from_xa, from_da, from_db, samples, hot, fit, design)

    got_xa = send_x(xa, 0)
    got_xb = send_x(xb, 1)
    got_db = send_across(db, 1)
    got_da = send_across(da, 0)
    za, zb = pl.pallas_call(
        relay_kernel,
        out_shape=(block(cx, REACH), block(cx, REACH)),
        in_specs=[VMEM] * 2,
        out_specs=(VMEM, VMEM),
        compiler_params=params(8),
        cost_estimate=SMALL,
        name="relay",
    )(total, got_xa)
    got_za = send_y(za, 0)
    got_zb = send_y(zb, 1)
    base, wide = pl.pallas_call(
        gather_kernel,
        out_shape=(block(cx, cy, kind=full), shape((cx, cy, depth, 128), full)),
        in_specs=[VMEM] * 6,
        out_specs=(VMEM, VMEM),
        compiler_params=params(12),
        cost_estimate=LARGE,
        name="gather",
    )(total, scale, got_xa, got_xb, got_za, got_zb)
    return pl.pallas_call(
        finish_kernel,
        out_shape=block(cx, cy),
        in_specs=[VMEM] * 4,
        out_specs=VMEM,
        compiler_params=params(12),
        cost_estimate=SMALL,
        name="finish",
    )(base, wide, got_da, got_db)


def solution(mesh):
    placed = (
        P("gx", "gy", None, None),
        P("gx", "gy", None, None, None),
        P("gx", "gy", None, None, None),
        P("gx", "gy", None, None),
        P("gx", "gy", None),
        P("gx", "gy", None, None),
        P("gx", "gy", None),
        P("gx", "gy", None),
    )
    return jax.shard_map(
        local, mesh=mesh, in_specs=placed, out_specs=P("gx", "gy", None, None), check_vma=False
    )
```

```python
import jax
import jax.numpy as jnp
from jax import lax
from jax.experimental import pallas as pl
from jax.experimental.pallas import tpu as pltpu
from jax.sharding import PartitionSpec as P

REACH = 4
SPAN = 2 * REACH + 1
LAYERS = 4
NEAR = 3
LOOKS = 2
EXPONENTS = (
    (0, 0, 0),
    (1, 0, 0),
    (0, 1, 0),
    (0, 0, 1),
    (2, 0, 0),
    (1, 1, 0),
    (1, 0, 1),
    (0, 2, 0),
    (0, 1, 1),
    (0, 0, 2),
    (3, 0, 0),
    (2, 1, 0),
    (2, 0, 1),
    (1, 2, 0),
    (1, 1, 1),
    (1, 0, 2),
    (0, 3, 0),
    (0, 2, 1),
    (0, 1, 2),
    (0, 0, 3),
)
DISTANCES = sorted({a * a + b * b for a in range(REACH + 1) for b in range(REACH + 1)})
SPOTS = [(ex, ey) for ex in range(SPAN) for ey in range(SPAN - 1)] + [(ex, SPAN - 1) for ex in range(SPAN)]
VMEM = pl.BlockSpec(memory_space=pltpu.VMEM)
SMEM = pl.BlockSpec(memory_space=pltpu.SMEM)


SMALL = pl.CostEstimate(flops=1000, bytes_accessed=1000, transcendentals=0)
LARGE = pl.CostEstimate(flops=4_000_000_000, bytes_accessed=40_000_000, transcendentals=0)


def up(value, multiple):
    return -(-value // multiple) * multiple


def parity():
    return lax.rem(lax.axis_index("gx"), 2), lax.rem(lax.axis_index("gy"), 2)


def partner(i, size, turn, wrap):
    j = i + 1 if i % 2 == turn else i - 1
    return j % size if wrap or 0 <= j < size else None


def routes(across, along, turn_x, turn_y):
    pairs = []
    for i in range(across):
        for j in range(along):
            to = i if turn_x is None else partner(i, across, turn_x, True)
            up_to = j if turn_y is None else partner(j, along, turn_y, False)
            if up_to is None:
                to, up_to = partner(i, across, 0, True), j
            pairs.append((i * along + j, to * along + up_to))
    return pairs


def paired(turn):
    j, odd = lax.axis_index("gy"), parity()[1]
    to = jnp.where(odd == turn, j + 1, j - 1)
    return jnp.where((to >= 0) & (to < lax.axis_size("gy")), 1.0, 0.0).astype(jnp.float32)


def pack_kernel(count, nodes_ref, *refs):
    plain, sent, copied, sems = refs[:count], refs[count : count + 6], refs[count + 6 : -1], refs[-1]
    ya_ref, yb_ref, xa_ref, xb_ref, da_ref, db_ref = sent
    sx, sy = nodes_ref.shape[:2]
    odd_x, odd_y = parity()
    far_x, back_x = (1 - odd_x) * (sx - 1), odd_x * (sx - 1)
    far_y, back_y = (1 - odd_y) * (sy - 1), odd_y * (sy - 1)
    pairs = (
        (nodes_ref.at[back_x, back_y], db_ref),
        (nodes_ref.at[back_x, far_y], da_ref),
        (nodes_ref.at[:, far_y], ya_ref),
        (nodes_ref.at[:, back_y], yb_ref),
        (nodes_ref.at[back_x], xb_ref),
        (nodes_ref.at[far_x], xa_ref),
        *zip(plain, copied),
    )
    copies = [pltpu.make_async_copy(source, target, sems.at[index]) for index, (source, target) in enumerate(pairs)]
    for copy in copies:
        copy.start()
    for copy in copies:
        copy.wait()


def extend_kernel(ya_ref, yb_ref, own_ref, out_ref):
    odd_x, odd_y = parity()
    far_x = (1 - odd_x) * (ya_ref.shape[0] - 1)
    last = out_ref.shape[0] - 1
    out_ref[1:last] = own_ref[...]
    out_ref[(1 - odd_y) * last] = ya_ref[far_x]
    out_ref[odd_y * last] = yb_ref[far_x]


def prepare_kernel(
    sides, subregion, tile, radius_ref, xyz_ref, cells_ref, valid_ref, nodes_ref, far_ref,
    design_ref, hot_ref, fit_ref, near_ref, split, places, sem, *scratch,
):
    slots, patches, unknowns = far_ref.shape
    copy = pltpu.make_async_copy(far_ref, near_ref, sem)
    copy.start()
    choose(sides, subregion, tile, cells_ref, valid_ref, nodes_ref, hot_ref, places)

    def also(p):
        if p == 0:
            copy.wait()
            spread(near_ref, split)
        turn(p, split, fit_ref, slots)

    design_kernel(slots, unknowns, radius_ref, xyz_ref, design_ref, also, *scratch)


def design_kernel(nodes, unknowns, radius_ref, xyz_ref, design_ref, also, pos, ax, by, ax2, bc, bm, bl, far):
    patches = design_ref.shape[0]
    lanes = design_ref.shape[2]
    tile = (2 * LAYERS, lanes)
    pos[:, :, 0:nodes] = xyz_ref[...]
    lane = lax.broadcasted_iota(jnp.int32, (1, lanes), 1)
    is_node = lane < nodes
    used = lane < unknowns
    power = []
    for axis in range(3):
        rows = []
        for degree in range(1, 4):
            hit = lane < 0
            for index, triple in enumerate(EXPONENTS):
                if triple[axis] == degree:
                    hit = hit | (lane == nodes + index)
            rows.append(hit)
        power.append(rows)

    def raised(value, axis):
        one, two, three = power[axis]
        square = value * value
        out = jnp.where(one, value, jnp.where(used, 1.0, 0.0))
        out = jnp.where(two, square, out)
        return jnp.where(three, square * value, out)

    across = (lax.broadcasted_iota(jnp.int32, (16, lanes), 0) - REACH).astype(jnp.float32)
    layer = lax.broadcasted_iota(jnp.int32, tile, 0)
    upper = layer < LAYERS
    deep = jnp.where(upper, layer, layer - LAYERS).astype(jnp.float32) - 0.5 * (LAYERS - 1)
    tail = slice(lanes - 128, lanes)
    half = SPAN // 2

    for index, flat in enumerate(DISTANCES):
        far[index] = jnp.sqrt(float(flat) + deep[:, :128] * deep[:, :128])

    def patch(p, q):
        inverse = 1.0 / jnp.full((1, lanes), radius_ref[0, p], jnp.float32)
        x = jnp.where(is_node, pos[0, pl.ds(p, 1), :], 0.0)
        y = jnp.where(is_node, pos[1, pl.ds(p, 1), :], 0.0)
        z = jnp.where(is_node, pos[2, pl.ds(p, 1), :], 0.0)
        dx = (across - x) * inverse
        dy = (across - y) * inverse
        dz = (deep - z) * inverse
        ax[q] = jnp.where(is_node, dx * dx, raised(dx, 0))
        by[q] = jnp.where(is_node, dy * dy, raised(dy, 1))
        cz = jnp.where(is_node, dz * dz + 1e-30, raised(dz, 2))
        for i in range(half + 1):
            low, high = 2 * i, min(2 * i + 1, SPAN - 1)
            row = jnp.where(upper, by[q, low : low + 1, :], by[q, high : high + 1, :])
            bc[q, i] = row + cz
            bm[q, i] = row[:, tail] * cz[:, tail]
            ax2[q, i] = jnp.where(upper, ax[q, low : low + 1, :], ax[q, high : high + 1, :])
        for index, flat in enumerate(DISTANCES):
            rho = far[index] * inverse[:, :128]
            left = jnp.maximum(1.0 - rho, 0.0)
            left = left * left
            bl[q, index] = left * left * (4.0 * rho + 1.0)

        def pair(spots):
            (ex, ey), (fx, fy) = spots[0], spots[-1]
            row = ax[q, ex : ex + 1, :] if ex == fx else ax2[q, ex // 2]
            part = row + bc[q, ey // 2]
            part = part * part * lax.rsqrt(part)
            last = row[:, tail] * bm[q, ey // 2]
            blend = [bl[q, DISTANCES.index((i - REACH) ** 2 + (j - REACH) ** 2)] for i, j in ((ex, ey), (fx, fy))]
            blend = blend[0] if (ex, ey) == (fx, fy) else jnp.where(upper[:, :128], blend[0], blend[1])
            if len(spots) == 1:
                blend = jnp.where(upper[:, :128], blend, 0.0)
            pieces = [part[:, c : c + 128] for c in range(0, lanes, 128)]
            pieces[-1] = jnp.where(is_node[:, tail], pieces[-1], last)
            return jnp.concatenate([piece * blend for piece in pieces], 1)

        for spot in range(0, len(SPOTS), 4):
            rows = [pair(SPOTS[r : r + 2]) if r < len(SPOTS) else jnp.zeros(tile, jnp.float32) for r in (spot, spot + 2)]
            design_ref[p, spot * LAYERS : (spot + 4) * LAYERS, :] = jnp.concatenate(rows, 0).astype(jnp.bfloat16)

    for p in range(patches):
        patch(p, p % LOOKS)
        also(p)


def spread(fit_ref, wide):
    slots, patches, unknowns = fit_ref.shape
    for c in range(0, unknowns, 128):
        width = min(128, unknowns - c)
        wide[c // 128, 0 : slots * patches, :width] = fit_ref[:, :, c : c + width].astype(jnp.float32).reshape(slots * patches, width)


def turn(p, wide, fit, slots):
    patches, unknowns, padded = fit.shape
    for c in range(0, unknowns, 128):
        width = min(128, unknowns - c)
        piece = wide[c // 128, pl.ds(p, slots, stride=patches), :].astype(fit.dtype)
        fit[p, c : c + width, 0:slots] = piece.T[:width]
        fit[p, c : c + width, slots:padded] = jnp.zeros((width, padded - slots), fit.dtype)


def choose(sides, subregion, tile, cells_ref, valid_ref, nodes_ref, hot, places):
    patches, slots = nodes_ref.shape
    padded = hot.shape[1]
    kind = hot.dtype
    lane = lax.broadcasted_iota(jnp.int32, (1, slots), 1)
    places[...] = jnp.full(places.shape, -1.0, jnp.float32)
    for p in range(patches):
        index = nodes_ref[p : p + 1, :]
        where = lax.div(index, jnp.int32(subregion))
        a = jnp.zeros_like(where)
        for t in range(1, sides[0] + 2):
            a = a + jnp.where(where >= t * (sides[1] + 2), 1, 0)
        b = where - a * (sides[1] + 2)
        home_x, home_y = home(sides, tile, cells_ref, p)
        local = (a - home_x) * NEAR + (b - home_y)
        local = jnp.where(lane < valid_ref[0, p], local, -1)
        places[0, p : p + 1, 0:slots] = (index - where * subregion).astype(jnp.float32)
        places[1, p : p + 1, 0:slots] = local.astype(jnp.float32)
    inner, local = places[0].T, places[1].T
    node = lax.broadcasted_iota(jnp.int32, (padded, subregion), 1).astype(jnp.float32).astype(kind)
    one, zero = jnp.ones((), kind), jnp.zeros((), kind)
    for p in range(patches):
        column = jnp.broadcast_to(inner[:padded, p : p + 1], (padded, subregion)).astype(kind)
        one_hot = jnp.where(node == column, one, zero)
        column = jnp.broadcast_to(local[:padded, p : p + 1], (padded, subregion)).astype(kind)
        for s in range(NEAR * NEAR):
            hot[p, :, s * subregion : (s + 1) * subregion] = jnp.where(column == jnp.full((), s, kind), one_hot, zero)


def home(sides, tile, cells_ref, p):
    return (cells_ref[0, 0, p] * sides[0]) // tile[0], (cells_ref[1, 0, p] * sides[1]) // tile[1]


def sample_kernel(
    tile, cells_ref, own_ref, b_ref, c_ref, d_ref, hot_ref, out_ref, near,
):
    sx, sy, subregion, fields = own_ref.shape
    odd_x, odd_y = parity()
    xa = (1 - odd_x) * (sx + 1)
    xb = odd_x * (sx + 1)
    ya = (1 - odd_y) * (sy + 1)
    yb = odd_y * (sy + 1)
    near[1 : sx + 1, 1 : sy + 1] = own_ref[...]
    near[xb, 1 : sy + 1] = b_ref[...]
    near[1 : sx + 1, ya] = c_ref[...]
    near[1 : sx + 1, yb] = d_ref[...]
    near[xb, ya] = jnp.zeros(near.shape[2:], near.dtype)
    near[xb, yb] = jnp.zeros(near.shape[2:], near.dtype)
    near[xa] = jnp.zeros(near.shape[1:], near.dtype)
    for p in range(hot_ref.shape[0]):
        home_x, home_y = home((sx, sy), tile, cells_ref, p)
        window = jnp.concatenate(
            [near[home_x + r, pl.ds(home_y, NEAR)].reshape(NEAR * subregion, fields) for r in range(NEAR)], 0
        )
        out_ref[p] = jnp.dot(hot_ref[p], window, preferred_element_type=jnp.float32).astype(out_ref.dtype)


def blend_kernel(
    sides, tile, cells_ref, side_ref, ea_ref, eb_ref, sample_ref, hot_ref, fit_ref, design_ref,
    acc, xa_ref, xb_ref, da_ref, db_ref, edges, chosen, coeffs, values,
):
    sx, sy = sides
    subregion, fields = side_ref.shape[1:]
    patches, unknowns, _ = fit_ref.shape
    cx, cy = tile
    rows = len(SPOTS) * LAYERS
    odd_x, odd_y = parity()
    xa, xb = (1 - odd_x) * (sx + 1), odd_x * (sx + 1)
    acc[...] = jnp.zeros_like(acc)
    edges[0] = side_ref[...]
    edges[1, 1 : sy + 1] = jnp.zeros((sy, subregion, fields), edges.dtype)
    edges[1, (1 - odd_y) * (sy + 1)] = ea_ref[...]
    edges[1, odd_y * (sy + 1)] = eb_ref[...]
    for p in range(patches):
        home_x, home_y = home(sides, tile, cells_ref, p)
        turn = jnp.where(jnp.abs(xa - home_x - 1) <= 1, 0, 1)
        row = jnp.where(turn == 0, xa, xb) - home_x
        here = (row >= 0) & (row < NEAR)
        spot = pl.multiple_of(jnp.where(here, row, 0) * (NEAR * subregion), NEAR * subregion)
        edge = edges[turn, pl.ds(home_y, NEAR)].reshape(NEAR * subregion, fields)
        edge = edge * jnp.where(here, 1.0, 0.0).astype(edge.dtype)
        extra = jnp.dot(hot_ref[p, :, pl.ds(spot, NEAR * subregion)], edge, preferred_element_type=jnp.float32)
        chosen[p] = sample_ref[p] + extra.astype(chosen.dtype)
    for p in range(patches):
        coeffs[p] = jnp.dot(fit_ref[p], chosen[p], preferred_element_type=jnp.float32).astype(coeffs.dtype)

    def place(p):
        first, second, third = cells_ref[0, 0, p], cells_ref[1, 0, p], cells_ref[2, 0, p]
        for s, (ex, ey) in enumerate(SPOTS):
            for l in range(acc.shape[0]):
                spot = (l, first + ex, second + ey, pl.ds(third, LAYERS))
                acc[spot] = acc[spot] + values[p, s * LAYERS : (s + 1) * LAYERS, l * 128 : (l + 1) * 128]

    for p in range(patches):
        values[p] = jnp.dot(design_ref[p, :rows, :unknowns], coeffs[p], preferred_element_type=jnp.float32)
        if p:
            place(p - 1)
    place(patches - 1)

    ra = (1 - odd_x) * (cx + REACH)
    rb = odd_x * (cx + REACH)
    sa = (1 - odd_y) * (cy + REACH)
    sb = odd_y * (cy + REACH)
    rim, in_y = REACH, pl.ds(REACH, cy)
    for l in range(acc.shape[0]):
        f = pl.ds(l * 128, 128)
        xa_ref[:, :, :, f] = acc[l, pl.ds(ra, rim)].astype(xa_ref.dtype)
        xb_ref[:, :, :, f] = acc[l, pl.ds(rb, rim), in_y].astype(xb_ref.dtype)
        for ref, s, turn in ((da_ref, sa, 0), (db_ref, sb, 1)):
            ref[:, :, :, f] = (acc[l, pl.ds(rb, rim), pl.ds(s, rim)] * paired(turn)).astype(ref.dtype)


def relay_kernel(acc_ref, xa_ref, outa_ref, outb_ref):
    odd_x, odd_y = parity()
    cx = outa_ref.shape[0]
    rows = pl.ds((1 - odd_x) * (cx - REACH), REACH)
    last = xa_ref.shape[1] - REACH
    for out_ref, s, turn in ((outa_ref, (1 - odd_y) * last, 0), (outb_ref, odd_y * last, 1)):
        keep = paired(turn)
        columns = pl.ds(s, REACH)
        for l in range(acc_ref.shape[0]):
            f = slice(l * 128, (l + 1) * 128)
            out_ref[:, :, :, f] = (acc_ref[l, pl.ds(REACH, cx), columns] * keep).astype(out_ref.dtype)
            mine = acc_ref[l, pl.ds((1 - odd_x) * (cx - REACH) + REACH, REACH), columns]
            got = xa_ref[:, columns, :, f].astype(jnp.float32)
            out_ref[rows, :, :, f] = ((mine + got) * keep).astype(out_ref.dtype)


def gather_kernel(acc_ref, scale_ref, xa_ref, xb_ref, za_ref, zb_ref, out_ref, wide_ref):
    cx, cy, depth, fields = out_ref.shape
    for i in range(cx):
        columns = scale_ref[i]
        for j in range(cy):
            wide_ref[i, j] = jnp.broadcast_to(columns[:, j : j + 1], wide_ref.shape[2:])
    odd_x, odd_y = parity()
    far, back = pl.ds((1 - odd_x) * (cx - REACH), REACH), pl.ds(odd_x * (cx - REACH), REACH)
    for f in range(0, fields, 128):
        part = slice(f, f + 128)
        out_ref[:, :, :, part] = acc_ref[f // 128, REACH : REACH + cx, REACH : REACH + cy] * wide_ref[...]
        got = xa_ref[:, REACH : REACH + cy, :, part].astype(jnp.float32)
        out_ref[far, :, :, part] = out_ref[far, :, :, part] + got * wide_ref[far]
        got = xb_ref[:, :, :, part].astype(jnp.float32)
        out_ref[back, :, :, part] = out_ref[back, :, :, part] + got * wide_ref[back]
        for z_ref, s in ((za_ref, (1 - odd_y) * (cy - REACH)), (zb_ref, odd_y * (cy - REACH))):
            spot = (slice(None), pl.ds(s, REACH))
            got = z_ref[:, :, :, part].astype(jnp.float32)
            out_ref[spot + (slice(None), part)] = out_ref[spot + (slice(None), part)] + got * wide_ref[spot]


def finish_kernel(base_ref, wide_ref, da_ref, db_ref, out_ref):
    cx, cy, depth, fields = base_ref.shape
    odd_x, odd_y = parity()
    back = pl.ds(odd_x * (cx - REACH), REACH)
    for f in range(0, fields, 128):
        part = slice(f, f + 128)
        out_ref[:, :, :, part] = base_ref[:, :, :, part].astype(out_ref.dtype)
        for d_ref, s in ((da_ref, (1 - odd_y) * (cy - REACH)), (db_ref, odd_y * (cy - REACH))):
            spot = (back, pl.ds(s, REACH))
            got = d_ref[:, :, :, part].astype(jnp.float32) * wide_ref[spot]
            out_ref[spot + (slice(None), part)] = (base_ref[spot + (slice(None), part)] + got).astype(out_ref.dtype)


def params(megabytes):
    return pltpu.CompilerParams(vmem_limit_bytes=megabytes * 2**20)


def local(node_values, fit_ops, node_xyz, patch_nodes, patch_valid, patch_cell, patch_radius, cell_scale):
    sx, sy, subregion, fields = node_values.shape
    patches, unknowns, slots = fit_ops.shape[2:]
    cx, cy, depth = cell_scale.shape
    across, along = lax.axis_size("gx"), lax.axis_size("gy")
    kind = node_values.dtype
    full = jnp.float32
    shape = jax.ShapeDtypeStruct
    lanes = up(unknowns, 128)
    rows = up(len(SPOTS), 4) * LAYERS
    halves = fields // 128

    def send(block, turn_x, turn_y):
        return lax.ppermute(block, ("gx", "gy"), routes(across, along, turn_x, turn_y))

    def send_x(block, turn):
        return send(block, turn, None)

    def send_y(block, turn):
        return send(block, None, turn)

    def send_across(block, turn):
        return send(block, 1, turn)

    line = lambda *sides: shape(sides + (subregion, fields), kind)
    plain = (
        patch_cell.transpose(0, 3, 1, 2)[0],
        patch_valid[0],
        patch_nodes[0, 0],
        patch_radius[0],
        node_xyz[0, 0].transpose(1, 0, 2),
        cell_scale.transpose(0, 2, 1),
    )
    packed = pl.pallas_call(
        lambda *refs: pack_kernel(len(plain), *refs),
        out_shape=(line(sx), line(sx), line(sy), line(sy), line(), line()) + tuple(shape(x.shape, x.dtype) for x in plain),
        in_specs=[pl.BlockSpec(memory_space=pl.ANY)] * (1 + len(plain)),
        out_specs=(VMEM,) * (6 + len(plain)),
        scratch_shapes=[pltpu.SemaphoreType.DMA((6 + len(plain),))],
        compiler_params=params(4),
        cost_estimate=SMALL,
        name="pack",
    )(*[pltpu.with_memory_space_constraint(x, pltpu.HBM) for x in (node_values, *plain)])
    to_ya, to_yb, to_xa, to_xb, to_da, to_db, cells, valid, indices, radius, xyz, scale = packed
    from_ya = send_y(to_ya, 0)
    from_yb = send_y(to_yb, 1)
    from_xb = send_x(to_xb, 1)
    from_da = send_across(to_da, 0)
    from_db = send_across(to_db, 1)
    window = NEAR * NEAR * subregion
    padded = up(slots, 16)
    far = pltpu.with_memory_space_constraint(fit_ops[0, 0].transpose(2, 0, 1), pltpu.HBM)
    design, hot, fit = pl.pallas_call(
        lambda *refs: prepare_kernel((sx, sy), subregion, (cx, cy), *refs),
        out_shape=(
            shape((patches, rows, lanes), kind),
            shape((patches, padded, window), kind),
            shape((patches, unknowns, padded), kind),
        ),
        in_specs=[SMEM, VMEM, SMEM, SMEM, VMEM, pl.BlockSpec(memory_space=pl.ANY)],
        out_specs=(VMEM,) * 3,
        scratch_shapes=[
            pltpu.VMEM(far.shape, kind),
            pltpu.VMEM((lanes // 128, padded * patches, 128), full),
            pltpu.VMEM((2, patches, up(padded, 128)), full),
            pltpu.SemaphoreType.DMA,
            pltpu.VMEM((3, patches, lanes), full),
            pltpu.VMEM((LOOKS, 16, lanes), full),
            pltpu.VMEM((LOOKS, 16, lanes), full),
            pltpu.VMEM((LOOKS, SPAN // 2 + 1, 2 * LAYERS, lanes), full),
            pltpu.VMEM((LOOKS, SPAN // 2 + 1, 2 * LAYERS, lanes), full),
            pltpu.VMEM((LOOKS, SPAN // 2 + 1, 2 * LAYERS, 128), full),
            pltpu.VMEM((LOOKS, len(DISTANCES), 2 * LAYERS, 128), full),
            pltpu.VMEM((len(DISTANCES), 2 * LAYERS, 128), full),
        ],
        compiler_params=params(24),
        cost_estimate=SMALL,
        name="prepare",
    )(radius, xyz, cells, valid, indices, far)
    from_xb, from_yb, from_ya, hot = lax.optimization_barrier((from_xb, from_yb, from_ya, hot))
    to_xa = pl.pallas_call(
        extend_kernel,
        out_shape=line(sy + 2),
        in_specs=[VMEM] * 3,
        out_specs=VMEM,
        compiler_params=params(4),
        cost_estimate=SMALL,
        name="extend",
    )(from_ya, from_yb, to_xa)
    from_xa = send_x(to_xa, 0)
    samples = pl.pallas_call(
        lambda *refs: sample_kernel((cx, cy), *refs),
        out_shape=shape((patches, padded, fields), kind),
        in_specs=[SMEM] + [VMEM] * 5,
        out_specs=VMEM,
        scratch_shapes=[pltpu.VMEM((sx + 2, sy + 2, subregion, fields), kind)],
        compiler_params=params(16),
        cost_estimate=LARGE,
        name="sample",
    )(cells, node_values, from_xb, from_ya, from_yb, hot)

    block = lambda *dims, kind=kind: shape(dims + (depth, fields), kind)
    total, xa, xb, da, db = pl.pallas_call(
        lambda *refs: blend_kernel((sx, sy), (cx, cy), *refs),
        out_shape=(
            shape((halves, cx + 2 * REACH + 1, cy + 2 * REACH, depth, 128), full),
            block(REACH, cy + 2 * REACH),
            block(REACH, cy),
            block(REACH, REACH),
            block(REACH, REACH),
        ),
        in_specs=[SMEM] + [VMEM] * 7,
        out_specs=(VMEM,) * 5,
        scratch_shapes=[
            pltpu.VMEM((2, sy + 2, subregion, fields), kind),
            pltpu.VMEM((patches, padded, fields), kind),
            pltpu.VMEM((patches, unknowns, fields), kind),
            pltpu.VMEM((patches, len(SPOTS) * LAYERS, fields), full),
        ],
        compiler_params=params(32),
        cost_estimate=SMALL,
        name="blend",
    )(cells, from_xa, from_da, from_db, samples, hot, fit, design)

    got_xa = send_x(xa, 0)
    got_xb = send_x(xb, 1)
    got_db = send_across(db, 1)
    got_da = send_across(da, 0)
    za, zb = pl.pallas_call(
        relay_kernel,
        out_shape=(block(cx, REACH), block(cx, REACH)),
        in_specs=[VMEM] * 2,
        out_specs=(VMEM, VMEM),
        compiler_params=params(8),
        cost_estimate=SMALL,
        name="relay",
    )(total, got_xa)
    got_za = send_y(za, 0)
    got_zb = send_y(zb, 1)
    base, wide = pl.pallas_call(
        gather_kernel,
        out_shape=(block(cx, cy, kind=full), shape((cx, cy, depth, 128), full)),
        in_specs=[VMEM] * 6,
        out_specs=(VMEM, VMEM),
        compiler_params=params(12),
        cost_estimate=LARGE,
        name="gather",
    )(total, scale, got_xa, got_xb, got_za, got_zb)
    return pl.pallas_call(
        finish_kernel,
        out_shape=block(cx, cy),
        in_specs=[VMEM] * 4,
        out_specs=VMEM,
        compiler_params=params(12),
        cost_estimate=SMALL,
        name="finish",
    )(base, wide, got_da, got_db)


def solution(mesh):
    placed = (
        P("gx", "gy", None, None),
        P("gx", "gy", None, None, None),
        P("gx", "gy", None, None, None),
        P("gx", "gy", None, None),
        P("gx", "gy", None),
        P("gx", "gy", None, None),
        P("gx", "gy", None),
        P("gx", "gy", None),
    )
    return jax.shard_map(
        local, mesh=mesh, in_specs=placed, out_specs=P("gx", "gy", None, None), check_vma=False
    )
```

```python
import jax
import jax.numpy as jnp
from jax import lax
from jax.experimental import pallas as pl
from jax.experimental.pallas import tpu as pltpu
from jax.sharding import PartitionSpec as P

REACH = 4
SPAN = 2 * REACH + 1
LAYERS = 4
NEAR = 3
LOOKS = 2
EXPONENTS = (
    (0, 0, 0),
    (1, 0, 0),
    (0, 1, 0),
    (0, 0, 1),
    (2, 0, 0),
    (1, 1, 0),
    (1, 0, 1),
    (0, 2, 0),
    (0, 1, 1),
    (0, 0, 2),
    (3, 0, 0),
    (2, 1, 0),
    (2, 0, 1),
    (1, 2, 0),
    (1, 1, 1),
    (1, 0, 2),
    (0, 3, 0),
    (0, 2, 1),
    (0, 1, 2),
    (0, 0, 3),
)
DISTANCES = sorted({a * a + b * b for a in range(REACH + 1) for b in range(REACH + 1)})
SPOTS = [(ex, ey) for ex in range(SPAN) for ey in range(SPAN - 1)] + [(ex, SPAN - 1) for ex in range(SPAN)]
VMEM = pl.BlockSpec(memory_space=pltpu.VMEM)
SMEM = pl.BlockSpec(memory_space=pltpu.SMEM)


SMALL = pl.CostEstimate(flops=1000, bytes_accessed=1000, transcendentals=0)
LARGE = pl.CostEstimate(flops=4_000_000_000, bytes_accessed=40_000_000, transcendentals=0)


def up(value, multiple):
    return -(-value // multiple) * multiple


def parity():
    return lax.rem(lax.axis_index("gx"), 2), lax.rem(lax.axis_index("gy"), 2)


def partner(i, size, turn, wrap):
    j = i + 1 if i % 2 == turn else i - 1
    return j % size if wrap or 0 <= j < size else None


def routes(across, along, turn_x, turn_y):
    pairs = []
    for i in range(across):
        for j in range(along):
            to = i if turn_x is None else partner(i, across, turn_x, True)
            up_to = j if turn_y is None else partner(j, along, turn_y, False)
            if up_to is None:
                to, up_to = partner(i, across, 0, True), j
            pairs.append((i * along + j, to * along + up_to))
    return pairs


def paired(turn):
    j, odd = lax.axis_index("gy"), parity()[1]
    to = jnp.where(odd == turn, j + 1, j - 1)
    return jnp.where((to >= 0) & (to < lax.axis_size("gy")), 1.0, 0.0).astype(jnp.float32)


def pack_kernel(count, nodes_ref, *refs):
    plain, sent, copied, sems = refs[:count], refs[count : count + 6], refs[count + 6 : -1], refs[-1]
    ya_ref, yb_ref, xa_ref, xb_ref, da_ref, db_ref = sent
    sx, sy = nodes_ref.shape[:2]
    odd_x, odd_y = parity()
    far_x, back_x = (1 - odd_x) * (sx - 1), odd_x * (sx - 1)
    far_y, back_y = (1 - odd_y) * (sy - 1), odd_y * (sy - 1)
    pairs = (
        (nodes_ref.at[back_x, back_y], db_ref),
        (nodes_ref.at[back_x, far_y], da_ref),
        (nodes_ref.at[:, far_y], ya_ref),
        (nodes_ref.at[:, back_y], yb_ref),
        (nodes_ref.at[back_x], xb_ref),
        (nodes_ref.at[far_x], xa_ref),
        *zip(plain, copied),
    )
    copies = [pltpu.make_async_copy(source, target, sems.at[index]) for index, (source, target) in enumerate(pairs)]
    for copy in copies:
        copy.start()
    for copy in copies:
        copy.wait()


def extend_kernel(ya_ref, yb_ref, own_ref, out_ref):
    odd_x, odd_y = parity()
    far_x = (1 - odd_x) * (ya_ref.shape[0] - 1)
    last = out_ref.shape[0] - 1
    out_ref[1:last] = own_ref[...]
    out_ref[(1 - odd_y) * last] = ya_ref[far_x]
    out_ref[odd_y * last] = yb_ref[far_x]


def prepare_kernel(
    sides, subregion, tile, radius_ref, xyz_ref, cells_ref, valid_ref, nodes_ref, far_ref,
    design_ref, hot_ref, fit_ref, near_ref, split, places, sem, *scratch,
):
    slots, patches, unknowns = far_ref.shape
    copy = pltpu.make_async_copy(far_ref, near_ref, sem)
    copy.start()
    choose(sides, subregion, tile, cells_ref, valid_ref, nodes_ref, hot_ref, places)

    def also(p):
        if p == 0:
            copy.wait()
            spread(near_ref, split)
        turn(p, split, fit_ref, slots)

    design_kernel(slots, unknowns, radius_ref, xyz_ref, design_ref, also, *scratch)


def design_kernel(nodes, unknowns, radius_ref, xyz_ref, design_ref, also, pos, ax, by, ax2, bc, bm, bl, far):
    patches = design_ref.shape[0]
    lanes = design_ref.shape[2]
    tile = (2 * LAYERS, lanes)
    pos[:, :, 0:nodes] = xyz_ref[...]
    lane = lax.broadcasted_iota(jnp.int32, (1, lanes), 1)
    is_node = lane < nodes
    used = lane < unknowns
    power = []
    for axis in range(3):
        rows = []
        for degree in range(1, 4):
            hit = lane < 0
            for index, triple in enumerate(EXPONENTS):
                if triple[axis] == degree:
                    hit = hit | (lane == nodes + index)
            rows.append(hit)
        power.append(rows)

    def raised(value, axis):
        one, two, three = power[axis]
        square = value * value
        out = jnp.where(one, value, jnp.where(used, 1.0, 0.0))
        out = jnp.where(two, square, out)
        return jnp.where(three, square * value, out)

    across = (lax.broadcasted_iota(jnp.int32, (16, lanes), 0) - REACH).astype(jnp.float32)
    layer = lax.broadcasted_iota(jnp.int32, tile, 0)
    upper = layer < LAYERS
    deep = jnp.where(upper, layer, layer - LAYERS).astype(jnp.float32) - 0.5 * (LAYERS - 1)
    tail = slice(lanes - 128, lanes)
    half = SPAN // 2

    for index, flat in enumerate(DISTANCES):
        far[index] = jnp.sqrt(float(flat) + deep[:, :128] * deep[:, :128])

    def patch(p, q):
        inverse = 1.0 / jnp.full((1, lanes), radius_ref[0, p], jnp.float32)
        x = jnp.where(is_node, pos[0, pl.ds(p, 1), :], 0.0)
        y = jnp.where(is_node, pos[1, pl.ds(p, 1), :], 0.0)
        z = jnp.where(is_node, pos[2, pl.ds(p, 1), :], 0.0)
        dx = (across - x) * inverse
        dy = (across - y) * inverse
        dz = (deep - z) * inverse
        ax[q] = jnp.where(is_node, dx * dx, raised(dx, 0))
        by[q] = jnp.where(is_node, dy * dy, raised(dy, 1))
        cz = jnp.where(is_node, dz * dz + 1e-30, raised(dz, 2))
        for i in range(half + 1):
            low, high = 2 * i, min(2 * i + 1, SPAN - 1)
            row = jnp.where(upper, by[q, low : low + 1, :], by[q, high : high + 1, :])
            bc[q, i] = row + cz
            bm[q, i] = row[:, tail] * cz[:, tail]
            ax2[q, i] = jnp.where(upper, ax[q, low : low + 1, :], ax[q, high : high + 1, :])
        for index, flat in enumerate(DISTANCES):
            rho = far[index] * inverse[:, :128]
            left = jnp.maximum(1.0 - rho, 0.0)
            left = left * left
            bl[q, index] = left * left * (4.0 * rho + 1.0)

        def pair(spots):
            (ex, ey), (fx, fy) = spots[0], spots[-1]
            row = ax[q, ex : ex + 1, :] if ex == fx else ax2[q, ex // 2]
            part = row + bc[q, ey // 2]
            part = part * part * lax.rsqrt(part)
            last = row[:, tail] * bm[q, ey // 2]
            blend = [bl[q, DISTANCES.index((i - REACH) ** 2 + (j - REACH) ** 2)] for i, j in ((ex, ey), (fx, fy))]
            blend = blend[0] if (ex, ey) == (fx, fy) else jnp.where(upper[:, :128], blend[0], blend[1])
            if len(spots) == 1:
                blend = jnp.where(upper[:, :128], blend, 0.0)
            pieces = [part[:, c : c + 128] for c in range(0, lanes, 128)]
            pieces[-1] = jnp.where(is_node[:, tail], pieces[-1], last)
            return jnp.concatenate([piece * blend for piece in pieces], 1)

        for spot in range(0, len(SPOTS), 4):
            rows = [pair(SPOTS[r : r + 2]) if r < len(SPOTS) else jnp.zeros(tile, jnp.float32) for r in (spot, spot + 2)]
            design_ref[p, spot * LAYERS : (spot + 4) * LAYERS, :] = jnp.concatenate(rows, 0).astype(jnp.bfloat16)

    for p in range(patches):
        patch(p, p % LOOKS)
        also(p)


def spread(fit_ref, wide):
    slots, patches, unknowns = fit_ref.shape
    for c in range(0, unknowns, 128):
        width = min(128, unknowns - c)
        wide[c // 128, 0 : slots * patches, :width] = fit_ref[:, :, c : c + width].astype(jnp.float32).reshape(slots * patches, width)


def turn(p, wide, fit, slots):
    patches, unknowns, padded = fit.shape
    for c in range(0, unknowns, 128):
        width = min(128, unknowns - c)
        piece = wide[c // 128, pl.ds(p, slots, stride=patches), :].astype(fit.dtype)
        fit[p, c : c + width, 0:slots] = piece.T[:width]
        fit[p, c : c + width, slots:padded] = jnp.zeros((width, padded - slots), fit.dtype)


def choose(sides, subregion, tile, cells_ref, valid_ref, nodes_ref, hot, places):
    patches, slots = nodes_ref.shape
    padded = hot.shape[1]
    kind = hot.dtype
    lane = lax.broadcasted_iota(jnp.int32, (1, slots), 1)
    places[...] = jnp.full(places.shape, -1.0, jnp.float32)
    for p in range(patches):
        index = nodes_ref[p : p + 1, :]
        where = lax.div(index, jnp.int32(subregion))
        a = jnp.zeros_like(where)
        for t in range(1, sides[0] + 2):
            a = a + jnp.where(where >= t * (sides[1] + 2), 1, 0)
        b = where - a * (sides[1] + 2)
        home_x, home_y = home(sides, tile, cells_ref, p)
        local = (a - home_x) * NEAR + (b - home_y)
        local = jnp.where(lane < valid_ref[0, p], local, -1)
        places[0, p : p + 1, 0:slots] = (index - where * subregion).astype(jnp.float32)
        places[1, p : p + 1, 0:slots] = local.astype(jnp.float32)
    inner, local = places[0].T, places[1].T
    node = lax.broadcasted_iota(jnp.int32, (padded, subregion), 1).astype(jnp.float32).astype(kind)
    one, zero = jnp.ones((), kind), jnp.zeros((), kind)
    for p in range(patches):
        column = jnp.broadcast_to(inner[:padded, p : p + 1], (padded, subregion)).astype(kind)
        one_hot = jnp.where(node == column, one, zero)
        column = jnp.broadcast_to(local[:padded, p : p + 1], (padded, subregion)).astype(kind)
        for s in range(NEAR * NEAR):
            hot[p, :, s * subregion : (s + 1) * subregion] = jnp.where(column == jnp.full((), s, kind), one_hot, zero)


def home(sides, tile, cells_ref, p):
    return (cells_ref[0, 0, p] * sides[0]) // tile[0], (cells_ref[1, 0, p] * sides[1]) // tile[1]


def sample_kernel(
    tile, cells_ref, own_ref, b_ref, c_ref, d_ref, hot_ref, out_ref, near,
):
    sx, sy, subregion, fields = own_ref.shape
    odd_x, odd_y = parity()
    xa = (1 - odd_x) * (sx + 1)
    xb = odd_x * (sx + 1)
    ya = (1 - odd_y) * (sy + 1)
    yb = odd_y * (sy + 1)
    near[1 : sx + 1, 1 : sy + 1] = own_ref[...]
    near[xb, 1 : sy + 1] = b_ref[...]
    near[1 : sx + 1, ya] = c_ref[...]
    near[1 : sx + 1, yb] = d_ref[...]
    near[xb, ya] = jnp.zeros(near.shape[2:], near.dtype)
    near[xb, yb] = jnp.zeros(near.shape[2:], near.dtype)
    near[xa] = jnp.zeros(near.shape[1:], near.dtype)
    for p in range(hot_ref.shape[0]):
        home_x, home_y = home((sx, sy), tile, cells_ref, p)
        window = jnp.concatenate(
            [near[home_x + r, pl.ds(home_y, NEAR)].reshape(NEAR * subregion, fields) for r in range(NEAR)], 0
        )
        out_ref[p] = jnp.dot(hot_ref[p], window, preferred_element_type=jnp.float32).astype(out_ref.dtype)


def blend_kernel(
    sides, tile, cells_ref, side_ref, ea_ref, eb_ref, sample_ref, hot_ref, fit_ref, design_ref,
    acc, xa_ref, xb_ref, da_ref, db_ref, edges, chosen, coeffs, values,
):
    sx, sy = sides
    subregion, fields = side_ref.shape[1:]
    patches, unknowns, _ = fit_ref.shape
    cx, cy = tile
    rows = len(SPOTS) * LAYERS
    odd_x, odd_y = parity()
    xa, xb = (1 - odd_x) * (sx + 1), odd_x * (sx + 1)
    acc[...] = jnp.zeros_like(acc)
    edges[0] = side_ref[...]
    edges[1, 1 : sy + 1] = jnp.zeros((sy, subregion, fields), edges.dtype)
    edges[1, (1 - odd_y) * (sy + 1)] = ea_ref[...]
    edges[1, odd_y * (sy + 1)] = eb_ref[...]
    for p in range(patches):
        home_x, home_y = home(sides, tile, cells_ref, p)
        turn = jnp.where(jnp.abs(xa - home_x - 1) <= 1, 0, 1)
        row = jnp.where(turn == 0, xa, xb) - home_x
        here = (row >= 0) & (row < NEAR)
        spot = pl.multiple_of(jnp.where(here, row, 0) * (NEAR * subregion), NEAR * subregion)
        edge = edges[turn, pl.ds(home_y, NEAR)].reshape(NEAR * subregion, fields)
        edge = edge * jnp.where(here, 1.0, 0.0).astype(edge.dtype)
        extra = jnp.dot(hot_ref[p, :, pl.ds(spot, NEAR * subregion)], edge, preferred_element_type=jnp.float32)
        chosen[p] = sample_ref[p] + extra.astype(chosen.dtype)
    for p in range(patches):
        coeffs[p] = jnp.dot(fit_ref[p], chosen[p], preferred_element_type=jnp.float32).astype(coeffs.dtype)

    def place(p):
        first, second, third = cells_ref[0, 0, p], cells_ref[1, 0, p], cells_ref[2, 0, p]
        for s, (ex, ey) in enumerate(SPOTS):
            for l in range(acc.shape[0]):
                spot = (l, first + ex, second + ey, pl.ds(third, LAYERS))
                acc[spot] = acc[spot] + values[p, s * LAYERS : (s + 1) * LAYERS, l * 128 : (l + 1) * 128]

    for p in range(patches):
        values[p] = jnp.dot(design_ref[p, :rows, :unknowns], coeffs[p], preferred_element_type=jnp.float32)
        if p:
            place(p - 1)
    place(patches - 1)

    ra = (1 - odd_x) * (cx + REACH)
    rb = odd_x * (cx + REACH)
    sa = (1 - odd_y) * (cy + REACH)
    sb = odd_y * (cy + REACH)
    rim, in_y = REACH, pl.ds(REACH, cy)
    for l in range(acc.shape[0]):
        f = pl.ds(l * 128, 128)
        xa_ref[:, :, :, f] = acc[l, pl.ds(ra, rim)].astype(xa_ref.dtype)
        xb_ref[:, :, :, f] = acc[l, pl.ds(rb, rim), in_y].astype(xb_ref.dtype)
        for ref, s, turn in ((da_ref, sa, 0), (db_ref, sb, 1)):
            ref[:, :, :, f] = (acc[l, pl.ds(rb, rim), pl.ds(s, rim)] * paired(turn)).astype(ref.dtype)


def relay_kernel(acc_ref, xa_ref, outa_ref, outb_ref):
    odd_x, odd_y = parity()
    cx = outa_ref.shape[0]
    rows = pl.ds((1 - odd_x) * (cx - REACH), REACH)
    last = xa_ref.shape[1] - REACH
    for out_ref, s, turn in ((outa_ref, (1 - odd_y) * last, 0), (outb_ref, odd_y * last, 1)):
        keep = paired(turn)
        columns = pl.ds(s, REACH)
        for l in range(acc_ref.shape[0]):
            f = slice(l * 128, (l + 1) * 128)
            out_ref[:, :, :, f] = (acc_ref[l, pl.ds(REACH, cx), columns] * keep).astype(out_ref.dtype)
            mine = acc_ref[l, pl.ds((1 - odd_x) * (cx - REACH) + REACH, REACH), columns]
            got = xa_ref[:, columns, :, f].astype(jnp.float32)
            out_ref[rows, :, :, f] = ((mine + got) * keep).astype(out_ref.dtype)


def gather_kernel(acc_ref, scale_ref, xa_ref, xb_ref, za_ref, zb_ref, out_ref, wide_ref):
    cx, cy, depth, fields = out_ref.shape
    for i in range(cx):
        columns = scale_ref[i]
        for j in range(cy):
            wide_ref[i, j] = jnp.broadcast_to(columns[:, j : j + 1], wide_ref.shape[2:])
    odd_x, odd_y = parity()
    far, back = pl.ds((1 - odd_x) * (cx - REACH), REACH), pl.ds(odd_x * (cx - REACH), REACH)
    for f in range(0, fields, 128):
        part = slice(f, f + 128)
        out_ref[:, :, :, part] = acc_ref[f // 128, REACH : REACH + cx, REACH : REACH + cy] * wide_ref[...]
        got = xa_ref[:, REACH : REACH + cy, :, part].astype(jnp.float32)
        out_ref[far, :, :, part] = out_ref[far, :, :, part] + got * wide_ref[far]
        got = xb_ref[:, :, :, part].astype(jnp.float32)
        out_ref[back, :, :, part] = out_ref[back, :, :, part] + got * wide_ref[back]
        for z_ref, s in ((za_ref, (1 - odd_y) * (cy - REACH)), (zb_ref, odd_y * (cy - REACH))):
            spot = (slice(None), pl.ds(s, REACH))
            got = z_ref[:, :, :, part].astype(jnp.float32)
            out_ref[spot + (slice(None), part)] = out_ref[spot + (slice(None), part)] + got * wide_ref[spot]


def finish_kernel(base_ref, wide_ref, da_ref, db_ref, out_ref, done, sems):
    cx, cy, depth, fields = base_ref.shape
    odd_x, odd_y = parity()
    far, back = pl.ds((1 - odd_x) * (cx - REACH), REACH), pl.ds(odd_x * (cx - REACH), REACH)
    copies = []
    for index, rows in enumerate((pl.ds(REACH, cx - 2 * REACH), far, back)):
        done[rows] = base_ref[rows].astype(done.dtype)
        if index == 2:
            for f in range(0, fields, 128):
                part = slice(f, f + 128)
                for d_ref, s in ((da_ref, (1 - odd_y) * (cy - REACH)), (db_ref, odd_y * (cy - REACH))):
                    spot = (back, pl.ds(s, REACH))
                    got = d_ref[:, :, :, part].astype(jnp.float32) * wide_ref[spot]
                    done[spot + (slice(None), part)] = (base_ref[spot + (slice(None), part)] + got).astype(done.dtype)
        copy = pltpu.make_async_copy(done.at[rows], out_ref.at[rows], sems.at[index])
        copy.start()
        copies.append(copy)
    for copy in copies:
        copy.wait()


def params(megabytes):
    return pltpu.CompilerParams(vmem_limit_bytes=megabytes * 2**20)


def local(node_values, fit_ops, node_xyz, patch_nodes, patch_valid, patch_cell, patch_radius, cell_scale):
    sx, sy, subregion, fields = node_values.shape
    patches, unknowns, slots = fit_ops.shape[2:]
    cx, cy, depth = cell_scale.shape
    across, along = lax.axis_size("gx"), lax.axis_size("gy")
    kind = node_values.dtype
    full = jnp.float32
    shape = jax.ShapeDtypeStruct
    lanes = up(unknowns, 128)
    rows = up(len(SPOTS), 4) * LAYERS
    halves = fields // 128

    def send(block, turn_x, turn_y):
        return lax.ppermute(block, ("gx", "gy"), routes(across, along, turn_x, turn_y))

    def send_x(block, turn):
        return send(block, turn, None)

    def send_y(block, turn):
        return send(block, None, turn)

    def send_across(block, turn):
        return send(block, 1, turn)

    line = lambda *sides: shape(sides + (subregion, fields), kind)
    plain = (
        patch_cell.transpose(0, 3, 1, 2)[0],
        patch_valid[0],
        patch_nodes[0, 0],
        patch_radius[0],
        node_xyz[0, 0].transpose(1, 0, 2),
        cell_scale.transpose(0, 2, 1),
    )
    packed = pl.pallas_call(
        lambda *refs: pack_kernel(len(plain), *refs),
        out_shape=(line(sx), line(sx), line(sy), line(sy), line(), line()) + tuple(shape(x.shape, x.dtype) for x in plain),
        in_specs=[pl.BlockSpec(memory_space=pl.ANY)] * (1 + len(plain)),
        out_specs=(VMEM,) * (6 + len(plain)),
        scratch_shapes=[pltpu.SemaphoreType.DMA((6 + len(plain),))],
        compiler_params=params(4),
        cost_estimate=SMALL,
        name="pack",
    )(*[pltpu.with_memory_space_constraint(x, pltpu.HBM) for x in (node_values, *plain)])
    to_ya, to_yb, to_xa, to_xb, to_da, to_db, cells, valid, indices, radius, xyz, scale = packed
    from_ya = send_y(to_ya, 0)
    from_yb = send_y(to_yb, 1)
    from_xb = send_x(to_xb, 1)
    from_da = send_across(to_da, 0)
    from_db = send_across(to_db, 1)
    window = NEAR * NEAR * subregion
    padded = up(slots, 16)
    far = pltpu.with_memory_space_constraint(fit_ops[0, 0].transpose(2, 0, 1), pltpu.HBM)
    design, hot, fit = pl.pallas_call(
        lambda *refs: prepare_kernel((sx, sy), subregion, (cx, cy), *refs),
        out_shape=(
            shape((patches, rows, lanes), kind),
            shape((patches, padded, window), kind),
            shape((patches, unknowns, padded), kind),
        ),
        in_specs=[SMEM, VMEM, SMEM, SMEM, VMEM, pl.BlockSpec(memory_space=pl.ANY)],
        out_specs=(VMEM,) * 3,
        scratch_shapes=[
            pltpu.VMEM(far.shape, kind),
            pltpu.VMEM((lanes // 128, padded * patches, 128), full),
            pltpu.VMEM((2, patches, up(padded, 128)), full),
            pltpu.SemaphoreType.DMA,
            pltpu.VMEM((3, patches, lanes), full),
            pltpu.VMEM((LOOKS, 16, lanes), full),
            pltpu.VMEM((LOOKS, 16, lanes), full),
            pltpu.VMEM((LOOKS, SPAN // 2 + 1, 2 * LAYERS, lanes), full),
            pltpu.VMEM((LOOKS, SPAN // 2 + 1, 2 * LAYERS, lanes), full),
            pltpu.VMEM((LOOKS, SPAN // 2 + 1, 2 * LAYERS, 128), full),
            pltpu.VMEM((LOOKS, len(DISTANCES), 2 * LAYERS, 128), full),
            pltpu.VMEM((len(DISTANCES), 2 * LAYERS, 128), full),
        ],
        compiler_params=params(24),
        cost_estimate=SMALL,
        name="prepare",
    )(radius, xyz, cells, valid, indices, far)
    from_xb, from_yb, from_ya, hot = lax.optimization_barrier((from_xb, from_yb, from_ya, hot))
    to_xa = pl.pallas_call(
        extend_kernel,
        out_shape=line(sy + 2),
        in_specs=[VMEM] * 3,
        out_specs=VMEM,
        compiler_params=params(4),
        cost_estimate=SMALL,
        name="extend",
    )(from_ya, from_yb, to_xa)
    from_xa = send_x(to_xa, 0)
    samples = pl.pallas_call(
        lambda *refs: sample_kernel((cx, cy), *refs),
        out_shape=shape((patches, padded, fields), kind),
        in_specs=[SMEM] + [VMEM] * 5,
        out_specs=VMEM,
        scratch_shapes=[pltpu.VMEM((sx + 2, sy + 2, subregion, fields), kind)],
        compiler_params=params(16),
        cost_estimate=LARGE,
        name="sample",
    )(cells, node_values, from_xb, from_ya, from_yb, hot)

    block = lambda *dims, kind=kind: shape(dims + (depth, fields), kind)
    total, xa, xb, da, db = pl.pallas_call(
        lambda *refs: blend_kernel((sx, sy), (cx, cy), *refs),
        out_shape=(
            shape((halves, cx + 2 * REACH + 1, cy + 2 * REACH, depth, 128), full),
            block(REACH, cy + 2 * REACH),
            block(REACH, cy),
            block(REACH, REACH),
            block(REACH, REACH),
        ),
        in_specs=[SMEM] + [VMEM] * 7,
        out_specs=(VMEM,) * 5,
        scratch_shapes=[
            pltpu.VMEM((2, sy + 2, subregion, fields), kind),
            pltpu.VMEM((patches, padded, fields), kind),
            pltpu.VMEM((patches, unknowns, fields), kind),
            pltpu.VMEM((patches, len(SPOTS) * LAYERS, fields), full),
        ],
        compiler_params=params(32),
        cost_estimate=SMALL,
        name="blend",
    )(cells, from_xa, from_da, from_db, samples, hot, fit, design)

    got_xa = send_x(xa, 0)
    got_xb = send_x(xb, 1)
    got_db = send_across(db, 1)
    got_da = send_across(da, 0)
    za, zb = pl.pallas_call(
        relay_kernel,
        out_shape=(block(cx, REACH), block(cx, REACH)),
        in_specs=[VMEM] * 2,
        out_specs=(VMEM, VMEM),
        compiler_params=params(8),
        cost_estimate=SMALL,
        name="relay",
    )(total, got_xa)
    got_za = send_y(za, 0)
    got_zb = send_y(zb, 1)
    base, wide = pl.pallas_call(
        gather_kernel,
        out_shape=(block(cx, cy, kind=full), shape((cx, cy, depth, 128), full)),
        in_specs=[VMEM] * 6,
        out_specs=(VMEM, VMEM),
        compiler_params=params(12),
        cost_estimate=LARGE,
        name="gather",
    )(total, scale, got_xa, got_xb, got_za, got_zb)
    return pl.pallas_call(
        finish_kernel,
        out_shape=block(cx, cy),
        in_specs=[VMEM] * 4,
        out_specs=pl.BlockSpec(memory_space=pl.ANY),
        scratch_shapes=[pltpu.VMEM((cx, cy, depth, fields), kind), pltpu.SemaphoreType.DMA((3,))],
        compiler_params=params(12),
        cost_estimate=SMALL,
        name="finish",
    )(base, wide, got_da, got_db)


def solution(mesh):
    placed = (
        P("gx", "gy", None, None),
        P("gx", "gy", None, None, None),
        P("gx", "gy", None, None, None),
        P("gx", "gy", None, None),
        P("gx", "gy", None),
        P("gx", "gy", None, None),
        P("gx", "gy", None),
        P("gx", "gy", None),
    )
    return jax.shard_map(
        local, mesh=mesh, in_specs=placed, out_specs=P("gx", "gy", None, None), check_vma=False
    )
```
